32 devices in a mesh: gx: 8 (over z, core), gy: 4 (over y, x).
Axes of the slice: x: 2, y: 2, z: 4, core: 2. Of those that a mesh axis runs over, the one named last changes fastest.
Arguments:
- water_state: float32 [3, 1024, 2048], P(None, 'gy', 'gx'), may hold values from -0.1 to 1, as said below
- ground: float32 [1024, 2048], P('gy', 'gx'), may hold values from 0 to 0.3
- log_rough: float32 [1024, 2048], P('gy', 'gx'), may hold values from -3.5 to -1.6
- moment: float32 [1024, 2048], P('gy', 'gx'), may hold values from -3 to 3
- second: float32 [1024, 2048], P('gy', 'gx'), may hold values from 0.001 to 1
- wet_tiles: int32 [8, 16], P('gy', 'gx'), may hold values from 0 to 1, as said below
- cotangent: float32 [3, 1024, 2048], P(None, 'gy', 'gx'), may hold values from -2400 to 2400
Outputs:
- new_rough: float32 [1024, 2048], P('gy', 'gx')
- new_moment: float32 [1024, 2048], P('gy', 'gx')
- new_second: float32 [1024, 2048], P('gy', 'gx')
The draws below stay inside these ranges and needn't reach their ends.
Inputs may be any that keep to these rules, and one draw needn't show every extreme that they name: `water_state`: depths (first field) lie in 0.2 to 1.0, discharges in -0.1 to 0.1. `wet_tiles`: two devices of one gy index whose gx indices differ by half of the gx axis form a pair; a pair holds at most 6 wet tiles together, and in every draw some pair holds exactly 6, one of its devices with all its tiles wet.
All inputs are finite; a program needn't handle non-finite values.
Results may differ from the reference program's by a relative error of at most 0.0003.
Values sent between devices are 32-bit elements; how exact they have to be, the bound alone decides.
A program may use at most 64 MiB of HBM per device.

```python
import math
import jax
import jax.numpy as jnp

TILE = 128
TR_DEV = 2
TC_DEV = 2
LOAD = 3
STEPS = 2
UPDATES = 20
ROWS = 1024
COLS = 2048
N_GX = 8
N_GY = 4


def draw_water_state(key, part):
    depth_key, flow_key = jax.random.split(key)
    depth_now = jax.random.uniform(depth_key, (ROWS, COLS), jnp.float32, minval=0.2, maxval=1.0)
    flows = jax.random.uniform(flow_key, (2, ROWS, COLS), jnp.float32, minval=-0.1, maxval=0.1)
    return jnp.concatenate([depth_now[None], flows], 0)


def draw_wet_tiles(key, part):
    tile_count = TR_DEV * TC_DEV
    half_axis = N_GX // 2
    heavy_key, light_key, side_key, score_key = jax.random.split(jax.random.fold_in(key, 7), 4)
    heavy = jax.random.randint(heavy_key, (N_GY, half_axis), LOAD, tile_count + 1)
    heavy = heavy.at[0, 0].set(tile_count)
    light = jax.random.randint(light_key, (N_GY, half_axis), 0, 2 * LOAD - heavy + 1)
    light = light.at[0, 0].set(2 * LOAD - tile_count)
    side = jax.random.randint(side_key, (N_GY, half_axis), 0, 2)
    lower = jnp.where(side > 0, heavy, light)
    upper = jnp.where(side > 0, light, heavy)
    counts = jnp.concatenate([lower, upper], 1)
    scores = jax.random.randint(score_key, (N_GY, N_GX, tile_count), 0, 1 << 20) * tile_count + jnp.arange(tile_count, dtype=jnp.int32)
    ranks = jnp.argsort(jnp.argsort(scores, axis=-1, stable=True), axis=-1, stable=True)
    wet = (ranks < counts[:, :, None]).astype(jnp.int32)
    wet = wet.reshape(N_GY, N_GX, TR_DEV, TC_DEV).transpose(0, 2, 1, 3)
    return wet.reshape(N_GY * TR_DEV, N_GX * TC_DEV)


def shard_levels(own_key, dims, cuts, smallest, high):
    def one(axis_at, parts):
        draws = jax.random.uniform(jax.random.fold_in(jax.random.fold_in(own_key, 6), axis_at), (parts,), jnp.float32, smallest / len(cuts), high / len(cuts))
        return jnp.repeat(jnp.exp(draws), dims[axis_at] // parts).reshape((-1,) + (1,) * (len(dims) - axis_at - 1))

    loudness = one(*cuts[0])
    for cut in cuts[1:]:
        loudness = loudness * one(*cut)
    return loudness


def scatter_about(stream_key, dims, deviation, most, shards=(), held_as=jnp.bfloat16):
    gain = shard_levels(stream_key, dims, shards, -0.22, 0.18) if shards else 1.0
    array = jax.random.normal(stream_key, dims, jnp.float32) * deviation * gain
    return jnp.minimum(jnp.maximum(array, -most), most).astype(held_as)


def setup_inputs(seed: int = 0) -> dict:
    arg_keys = jax.random.split(jax.random.key(seed), 8)
    return {
        "water_state": draw_water_state(jax.random.fold_in(arg_keys[7], 71), 0),
        "ground": jnp.clip(0.3 * jax.random.uniform(arg_keys[1], (ROWS, COLS), jnp.float32) ** shard_levels(arg_keys[1], (ROWS, COLS), ((0, 4), (1, 8)), -0.2, 0.2), 0.0, 0.3),
        "log_rough": jnp.clip(-3.5 + 1.9 * jax.random.uniform(arg_keys[2], (ROWS, COLS), jnp.float32) ** shard_levels(arg_keys[2], (ROWS, COLS), ((0, 4), (1, 8)), -0.2, 0.2), -3.5, -1.6),
        "moment": scatter_about(arg_keys[3], (ROWS, COLS), 0.5, 3.0, ((0, 4), (1, 8)), jnp.float32),
        "second": jnp.clip(jnp.exp(math.log(1.0) - 6.9077552 * jax.random.uniform(arg_keys[4], (ROWS, COLS), jnp.float32) ** shard_levels(arg_keys[4], (ROWS, COLS), ((0, 4), (1, 8)), -0.2, 0.2)), 0.001, 1.0),
        "wet_tiles": draw_wet_tiles(jax.random.fold_in(arg_keys[7], 71), 0),
        "cotangent": scatter_about(arg_keys[6], (3, ROWS, COLS), 400.0, 2400.0, ((1, 4), (2, 8)), jnp.float32),
    }


GRAVITY = 9.81
COURANT = 0.1
GRAVITY_DT = 9.81
SPEED_EPS = 0.0001
BETA_ONE = 0.9
BETA_TWO = 0.999
LEARN_RATE = 0.05
ATAN_SCALE = 1.27

def mirror_pad(water, ground):
    fields = jnp.concatenate([water, ground[None]], 0)
    padded = jnp.pad(fields, ((0, 0), (1, 1), (1, 1)), mode='edge')
    padded = padded.at[1, :, 0].multiply(-1.0).at[1, :, -1].multiply(-1.0)
    padded = padded.at[2, 0, :].multiply(-1.0).at[2, -1, :].multiply(-1.0)
    return padded

def mean_four(field):
    return 0.25 * (field[1:-1, 2:] + field[1:-1, :-2] + field[2:, 1:-1] + field[:-2, 1:-1])

def diff_cols(field):
    return field[:, 2:] - field[:, :-2]

def diff_rows(field):
    return field[2:, :] - field[:-2, :]

def flux_step(padded):
    depth_now, east_flow, south_flow, ground = (padded[0], padded[1], padded[2], padded[3])
    half_step = 0.5 * COURANT
    row_depth, row_east, row_south = (depth_now[1:-1, :], east_flow[1:-1, :], south_flow[1:-1, :])
    col_depth, col_east, col_south = (depth_now[:, 1:-1], east_flow[:, 1:-1], south_flow[:, 1:-1])
    inner_depth = depth_now[1:-1, 1:-1]
    new_depth = mean_four(depth_now) - half_step * (diff_cols(row_east) + diff_rows(col_south))
    new_east = mean_four(east_flow) - half_step * (diff_cols(row_east * row_east / row_depth + 0.5 * GRAVITY * row_depth * row_depth) + diff_rows(col_east * col_south / col_depth)) - half_step * GRAVITY * inner_depth * diff_cols(ground[1:-1, :])
    new_south = mean_four(south_flow) - half_step * (diff_cols(row_east * row_south / row_depth) + diff_rows(col_south * col_south / col_depth + 0.5 * GRAVITY * col_depth * col_depth)) - half_step * GRAVITY * inner_depth * diff_rows(ground[:, 1:-1])
    return jnp.stack([new_depth, new_east, new_south])

def friction(pre_state, log_rough):
    depth_now, east_flow, south_flow = (pre_state[0], pre_state[1], pre_state[2])
    speed = jnp.sqrt(east_flow * east_flow + south_flow * south_flow + SPEED_EPS)
    drag = 1.0 + GRAVITY_DT * jnp.exp(2.0 * log_rough) * speed * jnp.power(depth_now, -7.0 / 3.0)
    return jnp.stack([depth_now, east_flow / drag, south_flow / drag])

def forward(log_rough, water, ground, wet_cells):
    for step_index in range(STEPS):
        stepped = friction(flux_step(mirror_pad(water, ground)), log_rough)
        water = jnp.where(wet_cells[None], stepped, water)
    return water

def reference(water_state, ground, log_rough, moment, second, wet_tiles, cotangent):
    wet_cells = jnp.repeat(jnp.repeat(wet_tiles, TILE, 0), TILE, 1) > 0
    _, pullback = jax.vjp(lambda rough: forward(rough, water_state, ground, wet_cells), log_rough)
    gradient = pullback(cotangent)[0]
    new_moment = BETA_ONE * moment + (1.0 - BETA_ONE) * gradient
    new_second = BETA_TWO * second + (1.0 - BETA_TWO) * gradient * gradient
    direction = jnp.arctan2(new_moment / (1.0 - BETA_ONE ** UPDATES), jnp.sqrt(new_second / (1.0 - BETA_TWO ** UPDATES)))
    new_rough = log_rough - LEARN_RATE * ATAN_SCALE * direction
    return (new_rough, new_moment, new_second)
```

```python
import functools

import jax
import jax.numpy as jnp
from jax import lax
from jax.experimental import pallas as pl
from jax.experimental.pallas import tpu as pltpu
from jax.sharding import PartitionSpec as P

UPDATES = 20
GRAVITY = 9.81
HALF_STEP = 0.05
GRAVITY_DT = 9.81
SPEED_EPS = 0.0001
BETA_ONE = 0.9
BETA_TWO = 0.999
LEARN_RATE = 0.05
ATAN_SCALE = 1.27

MESH = pl.DeviceIdType.MESH
DEPTHS = (3, 3, 3, 3, 2, 1, 1, 1)
SEAMS = (3, 9, 15, 21, 26, 29, 31, 33)
PACK = 40
FLIP_X = (1, 6)
FLIP_Y = (2, 7)
LANES = 128
SUB = 8
CORNERS = ((-1, -1), (1, -1), (-1, 1), (1, 1))


def before_mask(shape):
    rows = lax.broadcasted_iota(jnp.int32, shape, 0)
    mask = jnp.zeros(shape, jnp.bool_)
    for seam, depth in zip(SEAMS, DEPTHS):
        mask = mask | ((rows >= seam - depth) & (rows < seam))
    return mask


def flip_signs(shape, flipped):
    rows = lax.broadcasted_iota(jnp.int32, shape, 0)
    mask = jnp.zeros(shape, jnp.bool_)
    for field in flipped:
        seam, depth = SEAMS[field], DEPTHS[field]
        mask = mask | ((rows >= seam - depth) & (rows < seam + depth))
    return jnp.where(mask, -1.0, 1.0)


def reflect_rows(src, dst, low, flipped):
    for field, (seam, depth) in enumerate(zip(SEAMS, DEPTHS)):
        sign = -1.0 if field in flipped else 1.0
        for j in range(depth):
            a, b = (seam - 1 - j, seam + j) if low else (seam + j, seam - 1 - j)
            dst[a : a + 1, :] = sign * src[b : b + 1, :]


def flux_parts(depth, east, south):
    inv = 1.0 / depth
    u, v = east * inv, south * inv
    press = (0.5 * GRAVITY) * depth * depth
    qh, qe, qs = 0.25 * depth, 0.25 * east, 0.25 * south
    a0 = HALF_STEP * east
    a1 = HALF_STEP * (east * u + press)
    a2 = HALF_STEP * (east * v)
    b0 = HALF_STEP * south
    b2 = HALF_STEP * (south * v + press)
    return u, v, (qh, qe, qs), (a0, a1, a2), (b0, a2, b2)


def kernel(
    n_gx,
    n_gy,
    water,
    ground,
    rough,
    wet,
    cot,
    grad_out,
    ext,
    rough_v,
    colpk,
    rowpk,
    corpk,
    col_in,
    row_in,
    cor_in,
    slopes,
    mix,
    rise,
    fall,
    state,
    damp,
    vel,
    lam,
    grad,
    load_sem,
    send_sem,
    recv_sem,
):
    side = rough.shape[0]
    width = rough.shape[1]
    tile_rows, tile_cols = wet.shape
    tile_h, tile_w = side // tile_rows, width // tile_cols
    ring = width + LANES
    chunks = side // SUB + 2
    gx = lax.axis_index("gx")
    gy = lax.axis_index("gy")

    def inside(dx, dy):
        checks = []
        if dx < 0:
            checks.append(gx > 0)
        if dx > 0:
            checks.append(gx < n_gx - 1)
        if dy < 0:
            checks.append(gy > 0)
        if dy > 0:
            checks.append(gy < n_gy - 1)
        return functools.reduce(jnp.logical_and, checks)

    def peer(dx, dy):
        return {"gx": gx + dx, "gy": gy + dy}

    loads = [
        pltpu.make_async_copy(water, ext.at[0:3, SUB : SUB + side, 0:width], load_sem.at[0]),
        pltpu.make_async_copy(rough, rough_v, load_sem.at[1]),
        pltpu.make_async_copy(ground, ext.at[3, SUB : SUB + side, 0:width], load_sem.at[2]),
        pltpu.make_async_copy(cot, ext.at[5:8, SUB : SUB + side, 0:width], load_sem.at[3]),
    ]
    for load in loads:
        load.start()

    barrier = pltpu.get_barrier_semaphore()
    around = [(dx, dy) for dx in (-1, 0, 1) for dy in (-1, 0, 1) if (dx, dy) != (0, 0)]
    count = jnp.int32(0)
    for dx, dy in around:
        ok = inside(dx, dy)

        @pl.when(ok)
        def _():
            pl.semaphore_signal(barrier, inc=1, device_id=peer(dx, dy), device_id_type=MESH)

        count = count + ok.astype(jnp.int32)

    for load in loads:
        load.wait()
    for i in range(tile_rows):
        for j in range(tile_cols):
            rs, cs = slice(i * tile_h, (i + 1) * tile_h), slice(j * tile_w, (j + 1) * tile_w)
            coef = GRAVITY_DT * jnp.exp(2.0 * rough_v[rs, cs])
            ext[4, SUB + i * tile_h : SUB + (i + 1) * tile_h, cs] = jnp.where(
                wet[i, j] > 0, coef, -1.0
            )

    for field, (seam, depth) in enumerate(zip(SEAMS, DEPTHS)):
        rowpk[seam - depth : seam, :] = ext[field, SUB + side - depth : SUB + side, 0:width]
        rowpk[seam : seam + depth, :] = ext[field, SUB : SUB + depth, 0:width]
    lane = lax.broadcasted_iota(jnp.int32, (PACK, LANES), 1)
    corpk[...] = jnp.where(lane < LANES // 2, rowpk[:, 0:LANES], rowpk[:, width - LANES : width])
    lane_b = lax.broadcasted_iota(jnp.int32, (LANES, LANES), 1)
    for b in range(side // LANES):
        packed = jnp.zeros((LANES, LANES), jnp.float32)
        rs = slice(SUB + b * LANES, SUB + (b + 1) * LANES)
        for field, (seam, depth) in enumerate(zip(SEAMS, DEPTHS)):
            both = jnp.where(
                lane_b < LANES // 2, ext[field, rs, 0:LANES], ext[field, rs, width - LANES : width]
            )
            both = pltpu.roll(both, seam, 1)
            packed = jnp.where((lane_b >= seam - depth) & (lane_b < seam + depth), both, packed)
        colpk[:, b * LANES : (b + 1) * LANES] = packed.T[0:PACK]

    pl.semaphore_wait(barrier, count)

    def straight(dx, dy, out_slot, in_slot):
        src, dst = (colpk, col_in) if dx else (rowpk, row_in)
        return pltpu.make_async_remote_copy(
            src_ref=src,
            dst_ref=dst.at[in_slot % 2],
            send_sem=send_sem.at[out_slot],
            recv_sem=recv_sem.at[in_slot],
            device_id=peer(dx, dy),
            device_id_type=MESH,
        )

    straights = [(-1, 0, 0, 1), (1, 0, 1, 0), (0, -1, 2, 3), (0, 1, 3, 2)]

    def corner(dx, dy, in_x, in_y, index):
        slot = CORNERS.index((-dx if in_x else dx, -dy if in_y else dy))
        return pltpu.make_async_remote_copy(
            src_ref=corpk,
            dst_ref=cor_in.at[slot],
            send_sem=send_sem.at[4 + index],
            recv_sem=recv_sem.at[4 + slot],
            device_id=peer(dx if in_x else 0, dy if in_y else 0),
            device_id_type=MESH,
        )

    def corner_cases(index):
        dx, dy = CORNERS[index]
        ok_x, ok_y = inside(dx, 0), inside(0, dy)
        no_x, no_y = jnp.logical_not(ok_x), jnp.logical_not(ok_y)
        return [
            (ok_x & ok_y, corner(dx, dy, True, True, index)),
            (ok_x & no_y, corner(dx, dy, True, False, index)),
            (no_x & ok_y, corner(dx, dy, False, True, index)),
        ]

    for args in straights:

        @pl.when(inside(args[0], args[1]))
        def _():
            straight(*args).start()

    for index in range(4):
        for ok, copy in corner_cases(index):

            @pl.when(ok)
            def _():
                copy.start()

        dx, dy = CORNERS[index]

        @pl.when(jnp.logical_not(inside(dx, 0) | inside(0, dy)))
        def _():
            cor_in[index] = corpk[...]

    for slot, (dx, dy) in enumerate(((-1, 0), (1, 0), (0, -1), (0, 1))):

        @pl.when(jnp.logical_not(inside(dx, dy)))
        def _():
            if dx:
                reflect_rows(colpk, col_in.at[slot % 2], dx < 0, FLIP_X)
            else:
                reflect_rows(rowpk, row_in.at[slot % 2], dy < 0, FLIP_Y)

    for args in straights:

        @pl.when(inside(args[0], args[1]))
        def _():
            dx, dy, out_slot, _ = args
            back = straight(dx, dy, out_slot, out_slot)
            back.wait_send()
            back.wait_recv()

    for index in range(4):
        dx, dy = CORNERS[index]

        @pl.when(inside(dx, 0) | inside(0, dy))
        def _():
            copy = pltpu.make_async_remote_copy(
                src_ref=corpk,
                dst_ref=cor_in.at[index],
                send_sem=send_sem.at[4 + index],
                recv_sem=recv_sem.at[4 + index],
                device_id=peer(0, 0),
                device_id_type=MESH,
            )
            copy.wait_send()
            copy.wait_recv()

        @pl.when(jnp.logical_not(inside(0, dy)))
        def _():
            reflect_rows(cor_in.at[index], cor_in.at[index], dy < 0, FLIP_Y)

        @pl.when(jnp.logical_not(inside(dx, 0)))
        def _():
            block = cor_in[index]
            turned = block
            for j in range(max(DEPTHS)):
                if dx < 0:
                    moved = pltpu.roll(block, LANES - 1 - 2 * j, 1)
                    turned = jnp.where(lane == LANES - 1 - j, moved, turned)
                else:
                    moved = pltpu.roll(block, 2 * j + 1, 1)
                    turned = jnp.where(lane == j, moved, turned)
            cor_in[index] = turned * flip_signs((PACK, LANES), FLIP_X)

    low_w = before_mask((PACK, LANES))
    for b in range(side // LANES):
        cs = slice(b * LANES, (b + 1) * LANES)
        halo = jnp.where(low_w, col_in[0, :, cs], col_in[1, :, cs])
        halo = jnp.concatenate([halo, jnp.zeros((LANES - PACK, LANES), jnp.float32)], 0).T
        for field, seam in enumerate(SEAMS):
            ext[field, SUB + b * LANES : SUB + (b + 1) * LANES, width:ring] = pltpu.roll(
                halo, LANES - seam, 1
            )
    for field, (seam, depth) in enumerate(zip(SEAMS, DEPTHS)):
        north, south = slice(seam - depth, seam), slice(seam, seam + depth)
        top, end = slice(SUB - depth, SUB), slice(SUB + side, SUB + side + depth)
        ext[field, top, 0:width] = row_in[0, north, :]
        ext[field, end, 0:width] = row_in[1, south, :]
        east_lane = lax.broadcasted_iota(jnp.int32, (depth, LANES), 1) < LANES // 2
        ext[field, top, width:ring] = jnp.where(east_lane, cor_in[1, north], cor_in[0, north])
        ext[field, end, width:ring] = jnp.where(east_lane, cor_in[3, south], cor_in[2, south])

    def start_of(chunk):
        return chunk * SUB if isinstance(chunk, int) else pl.multiple_of(chunk * SUB, SUB)

    def beside(ref, lead, chunk, shift, columns=slice(None)):
        view = ref.at[lead + (pl.ds(start_of(chunk), 3 * SUB),)]
        return view[SUB + shift : 2 * SUB + shift, columns]

    def east_of(array):
        return pltpu.roll(array, ring - 1, 1)

    def west_of(array):
        return pltpu.roll(array, 1, 1)

    def spread(step, chunk, values):
        at = start_of(chunk)
        u, v, quarter, a, b = flux_parts(*values)
        for f in range(3):
            mix[step, f, pl.ds(at, SUB), :] = east_of(quarter[f] - a[f]) + west_of(quarter[f] + a[f])
            rise[step, f, pl.ds(at + SUB, SUB), :] = quarter[f] - b[f]
            fall[step, f, pl.ds(at + SUB, SUB), :] = quarter[f] + b[f]
        return u, v

    def gather(step, chunk, depth, slope_x, slope_y):
        at = start_of(chunk)
        pre = [
            mix[step, f, pl.ds(at, SUB), :]
            + beside(rise, (step, f), chunk, 1)
            + beside(fall, (step, f), chunk, -1)
            for f in range(3)
        ]
        return pre[0], pre[1] - depth * slope_x, pre[2] - depth * slope_y

    def drag_of(coef, pre):
        depth, east, south = pre
        square = east * east + south * south + SPEED_EPS
        inv_speed = lax.rsqrt(square)
        power = jnp.exp((-7.0 / 3.0) * jnp.log(depth))
        extra = coef * (square * inv_speed) * power
        return extra, 1.0 / (1.0 + extra), inv_speed * inv_speed

    def stage_one(chunk):
        at = start_of(chunk)
        z = ext[3, pl.ds(at, SUB), :]
        scale = HALF_STEP * GRAVITY
        slopes[0, pl.ds(at, SUB), :] = scale * (east_of(z) - west_of(z))
        rise[0, 3, pl.ds(at + SUB, SUB), :] = scale * z
        spread(0, chunk, [ext[f, pl.ds(at, SUB), :] for f in range(3)])

    def stage_two(chunk):
        at = start_of(chunk)
        rows = pl.ds(at, SUB)
        depth, east, south = [ext[f, rows, :] for f in range(3)]
        slope_y = (
            beside(rise, (0, 3), chunk, 1) - beside(rise, (0, 3), chunk, -1)
        )
        slopes[1, rows, :] = slope_y
        pre = gather(0, chunk, depth, slopes[0, rows, :], slope_y)
        coef = ext[4, rows, :]
        is_wet = coef > 0
        extra, inv, _ = drag_of(coef, pre)
        now = [
            jnp.where(is_wet, pre[0], depth),
            jnp.where(is_wet, pre[1] * inv, east),
            jnp.where(is_wet, pre[2] * inv, south),
        ]
        damp[rows, :] = (extra * inv)[:, 0:width]
        for f in range(3):
            state[f, rows, :] = now[f]
        u, v = spread(1, chunk, now)
        vel[0, rows, :] = u[:, 0:width]
        vel[1, rows, :] = v[:, 0:width]

    def stage_three(chunk):
        at = start_of(chunk)
        rows = pl.ds(at, SUB)
        pre = gather(1, chunk, state[0, rows, :], slopes[0, rows, :], slopes[1, rows, :])
        coef = ext[4, rows, :]
        is_wet = coef > 0
        extra, inv, inv_square = drag_of(coef, pre)
        c_depth, c_east, c_south = [ext[5 + f, rows, :] for f in range(3)]
        t = -(c_east * pre[1] + c_south * pre[2]) * (inv * inv * extra)
        lam_rows = pl.ds(at + SUB, SUB)
        tq = t * inv_square
        lam[0, lam_rows, :] = jnp.where(is_wet, c_depth - (7.0 / 3.0) * t / pre[0], 0.0)
        lam[1, lam_rows, :] = jnp.where(is_wet, c_east * inv + tq * pre[1], 0.0)
        lam[2, lam_rows, :] = jnp.where(is_wet, c_south * inv + tq * pre[2], 0.0)
        grad[rows, :] = t[:, 0:width]

    def stage_four(chunk):
        at = start_of(chunk)
        rows = pl.ds(at, SUB)
        mean, dx, dy = [], [], []
        for f in range(3):
            here = lam[f, pl.ds(at + SUB, SUB), :]
            east = east_of(here)[:, 0:width]
            west = west_of(here)[:, 0:width]
            south = beside(lam, (f,), chunk, 1, slice(0, width))
            north = beside(lam, (f,), chunk, -1, slice(0, width))
            if f:
                mean.append(0.25 * ((east + west) + (south + north)))
            dx.append(HALF_STEP * (east - west))
            dy.append(HALF_STEP * (south - north))
        u, v = vel[0, rows, :], vel[1, rows, :]
        cross = dx[2] + dy[1]
        a_east = mean[0] + dx[0] + 2.0 * u * dx[1] + v * cross
        a_south = mean[1] + dy[0] + 2.0 * v * dy[2] + u * cross
        total = grad[rows, :] - (
            a_east * state[1, rows, 0:width] + a_south * state[2, rows, 0:width]
        ) * damp[rows, :]
        is_wet = ext[4, rows, 0:width] > 0
        out = at - SUB if isinstance(chunk, int) else pl.multiple_of(at - SUB, SUB)
        grad_out[pl.ds(out, SUB), :] = jnp.where(is_wet, 2.0 * total, 0.0)

    stages = (
        (6, stage_four, 1, chunks - 1),
        (4, stage_three, 0, chunks),
        (2, stage_two, 0, chunks),
        (0, stage_one, 0, chunks),
    )

    def turn(i):
        for lag, stage, low, high in stages:
            if not isinstance(i, int) or low <= i - lag < high:
                stage(i - lag)

    first = 7
    for i in range(first):
        turn(i)

    def body(i, carry):
        turn(i)
        return carry

    lax.fori_loop(first, chunks, body, 0)
    for i in range(chunks, chunks + 6):
        turn(i)


def on_device(n_gx, n_gy, water_state, ground, log_rough, moment, second, wet_tiles, cotangent):
    side, width = ground.shape
    ring = width + LANES
    rows = side + 2 * SUB
    tall = rows + 2 * SUB
    f32 = jnp.float32
    anywhere = pl.BlockSpec(memory_space=pl.ANY)
    gradient = pl.pallas_call(
        functools.partial(kernel, n_gx, n_gy),
        out_shape=jax.ShapeDtypeStruct((side, width), f32),
        in_specs=[anywhere, anywhere, anywhere, pl.BlockSpec(memory_space=pltpu.SMEM), anywhere],
        out_specs=pl.BlockSpec(memory_space=pltpu.VMEM),
        scratch_shapes=[
            pltpu.VMEM((8, rows, ring), f32),
            pltpu.VMEM((side, width), f32),
            pltpu.VMEM((PACK, side), f32),
            pltpu.VMEM((PACK, width), f32),
            pltpu.VMEM((PACK, LANES), f32),
            pltpu.VMEM((2, PACK, side), f32),
            pltpu.VMEM((2, PACK, width), f32),
            pltpu.VMEM((4, PACK, LANES), f32),
            pltpu.VMEM((2, rows, ring), f32),
            pltpu.VMEM((2, 3, rows, ring), f32),
            pltpu.VMEM((2, 4, tall, ring), f32),
            pltpu.VMEM((2, 3, tall, ring), f32),
            pltpu.VMEM((3, rows, ring), f32),
            pltpu.VMEM((rows, width), f32),
            pltpu.VMEM((2, rows, width), f32),
            pltpu.VMEM((3, tall, ring), f32),
            pltpu.VMEM((rows, width), f32),
            pltpu.SemaphoreType.DMA((4,)),
            pltpu.SemaphoreType.DMA((8,)),
            pltpu.SemaphoreType.DMA((8,)),
        ],
        compiler_params=pltpu.CompilerParams(
            collective_id=0, has_side_effects=True, vmem_limit_bytes=48 * 1024 * 1024
        ),
        name="flood_gradient",
    )(water_state, ground, log_rough, wet_tiles, cotangent)
    new_moment = BETA_ONE * moment + (1.0 - BETA_ONE) * gradient
    new_second = BETA_TWO * second + (1.0 - BETA_TWO) * gradient * gradient
    direction = jnp.arctan2(
        new_moment / (1.0 - BETA_ONE**UPDATES), jnp.sqrt(new_second / (1.0 - BETA_TWO**UPDATES))
    )
    new_rough = log_rough - LEARN_RATE * ATAN_SCALE * direction
    return (new_rough, new_moment, new_second)


def solution(mesh):
    field, plane = P(None, "gy", "gx"), P("gy", "gx")
    return jax.shard_map(
        functools.partial(on_device, mesh.shape["gx"], mesh.shape["gy"]),
        mesh=mesh,
        in_specs=(field, plane, plane, plane, plane, plane, field),
        out_specs=(plane, plane, plane),
        check_vma=False,
    )
```

```python
import functools

import jax
import jax.numpy as jnp
from jax import lax
from jax.experimental import pallas as pl
from jax.experimental.pallas import tpu as pltpu
from jax.sharding import PartitionSpec as P

UPDATES = 20
GRAVITY = 9.81
HALF_STEP = 0.05
GRAVITY_DT = 9.81
SPEED_EPS = 0.0001
BETA_ONE = 0.9
BETA_TWO = 0.999
LEARN_RATE = 0.05
ATAN_SCALE = 1.27

MESH = pl.DeviceIdType.MESH
DEPTHS = (3, 3, 3, 3, 2, 1, 1, 1)
SEAMS = (3, 9, 15, 21, 26, 29, 31, 33)
PACK = 40
FLIP_X = (1, 6)
FLIP_Y = (2, 7)
LANES = 128
SUB = 8
CORNERS = ((-1, -1), (1, -1), (-1, 1), (1, 1))


def before_mask(shape):
    rows = lax.broadcasted_iota(jnp.int32, shape, 0)
    mask = jnp.zeros(shape, jnp.bool_)
    for seam, depth in zip(SEAMS, DEPTHS):
        mask = mask | ((rows >= seam - depth) & (rows < seam))
    return mask


def flip_signs(shape, flipped):
    rows = lax.broadcasted_iota(jnp.int32, shape, 0)
    mask = jnp.zeros(shape, jnp.bool_)
    for field in flipped:
        seam, depth = SEAMS[field], DEPTHS[field]
        mask = mask | ((rows >= seam - depth) & (rows < seam + depth))
    return jnp.where(mask, -1.0, 1.0)


def reflect_rows(src, dst, low, flipped):
    for field, (seam, depth) in enumerate(zip(SEAMS, DEPTHS)):
        sign = -1.0 if field in flipped else 1.0
        for j in range(depth):
            a, b = (seam - 1 - j, seam + j) if low else (seam + j, seam - 1 - j)
            dst[a : a + 1, :] = sign * src[b : b + 1, :]


def inverse(x):
    guess = pl.reciprocal(x, approx=True)
    return guess * (2.0 - x * guess)


def flux_parts(depth, east, south):
    inv = inverse(depth)
    u, v = east * inv, south * inv
    press = (0.5 * GRAVITY) * depth * depth
    qh, qe, qs = 0.25 * depth, 0.25 * east, 0.25 * south
    a0 = HALF_STEP * east
    a1 = HALF_STEP * (east * u + press)
    a2 = HALF_STEP * (east * v)
    b0 = HALF_STEP * south
    b2 = HALF_STEP * (south * v + press)
    return u, v, (qh, qe, qs), (a0, a1, a2), (b0, a2, b2)


def kernel(
    n_gx,
    n_gy,
    water,
    ground,
    rough,
    wet_tiles,
    cot,
    grad_out,
    wet,
    ext,
    rough_v,
    colpk,
    rowpk,
    corpk,
    col_in,
    row_in,
    cor_in,
    slopes,
    mix,
    rise,
    fall,
    state,
    damp,
    vel,
    lam,
    grad,
    load_sem,
    send_sem,
    recv_sem,
):
    side = rough.shape[0]
    width = rough.shape[1]
    tile_rows, tile_cols = wet.shape
    tile_h, tile_w = side // tile_rows, width // tile_cols
    ring = width + LANES
    chunks = side // SUB + 2
    gx = lax.axis_index("gx")
    gy = lax.axis_index("gy")

    def inside(dx, dy):
        checks = []
        if dx < 0:
            checks.append(gx > 0)
        if dx > 0:
            checks.append(gx < n_gx - 1)
        if dy < 0:
            checks.append(gy > 0)
        if dy > 0:
            checks.append(gy < n_gy - 1)
        return functools.reduce(jnp.logical_and, checks)

    def peer(dx, dy):
        return {"gx": gx + dx, "gy": gy + dy}

    loads = [
        pltpu.make_async_copy(water, ext.at[0:3, SUB : SUB + side, 0:width], load_sem.at[0]),
        pltpu.make_async_copy(rough, rough_v, load_sem.at[1]),
        pltpu.make_async_copy(ground, ext.at[3, SUB : SUB + side, 0:width], load_sem.at[2]),
        pltpu.make_async_copy(cot, ext.at[5:8, SUB : SUB + side, 0:width], load_sem.at[3]),
        pltpu.make_async_copy(wet_tiles, wet, load_sem.at[4]),
    ]
    for load in loads:
        load.start()

    barrier = pltpu.get_barrier_semaphore()
    around = [(dx, dy) for dx in (-1, 0, 1) for dy in (-1, 0, 1) if (dx, dy) != (0, 0)]
    count = jnp.int32(0)
    for dx, dy in around:
        ok = inside(dx, dy)

        @pl.when(ok)
        def _():
            pl.semaphore_signal(barrier, inc=1, device_id=peer(dx, dy), device_id_type=MESH)

        count = count + ok.astype(jnp.int32)

    for load in loads:
        load.wait()
    for i in range(tile_rows):
        for j in range(tile_cols):
            rs, cs = slice(i * tile_h, (i + 1) * tile_h), slice(j * tile_w, (j + 1) * tile_w)
            coef = GRAVITY_DT * jnp.exp(2.0 * rough_v[rs, cs])
            ext[4, SUB + i * tile_h : SUB + (i + 1) * tile_h, cs] = jnp.where(
                wet[i, j] > 0, coef, -1.0
            )

    for field, (seam, depth) in enumerate(zip(SEAMS, DEPTHS)):
        rowpk[seam - depth : seam, :] = ext[field, SUB + side - depth : SUB + side, 0:width]
        rowpk[seam : seam + depth, :] = ext[field, SUB : SUB + depth, 0:width]
    lane = lax.broadcasted_iota(jnp.int32, (PACK, LANES), 1)
    corpk[...] = jnp.where(lane < LANES // 2, rowpk[:, 0:LANES], rowpk[:, width - LANES : width])
    lane_b = lax.broadcasted_iota(jnp.int32, (LANES, LANES), 1)
    for b in range(side // LANES):
        packed = jnp.zeros((LANES, LANES), jnp.float32)
        rs = slice(SUB + b * LANES, SUB + (b + 1) * LANES)
        for field, (seam, depth) in enumerate(zip(SEAMS, DEPTHS)):
            both = jnp.where(
                lane_b < LANES // 2, ext[field, rs, 0:LANES], ext[field, rs, width - LANES : width]
            )
            both = pltpu.roll(both, seam, 1)
            packed = jnp.where((lane_b >= seam - depth) & (lane_b < seam + depth), both, packed)
        colpk[:, b * LANES : (b + 1) * LANES] = packed.T[0:PACK]

    pl.semaphore_wait(barrier, count)

    def straight(dx, dy, out_slot, in_slot):
        src, dst = (colpk, col_in) if dx else (rowpk, row_in)
        return pltpu.make_async_remote_copy(
            src_ref=src,
            dst_ref=dst.at[in_slot % 2],
            send_sem=send_sem.at[out_slot],
            recv_sem=recv_sem.at[in_slot],
            device_id=peer(dx, dy),
            device_id_type=MESH,
        )

    straights = [(-1, 0, 0, 1), (1, 0, 1, 0), (0, -1, 2, 3), (0, 1, 3, 2)]

    def corner(dx, dy, in_x, in_y, index):
        slot = CORNERS.index((-dx if in_x else dx, -dy if in_y else dy))
        return pltpu.make_async_remote_copy(
            src_ref=corpk,
            dst_ref=cor_in.at[slot],
            send_sem=send_sem.at[4 + index],
            recv_sem=recv_sem.at[4 + slot],
            device_id=peer(dx if in_x else 0, dy if in_y else 0),
            device_id_type=MESH,
        )

    def corner_cases(index):
        dx, dy = CORNERS[index]
        ok_x, ok_y = inside(dx, 0), inside(0, dy)
        no_x, no_y = jnp.logical_not(ok_x), jnp.logical_not(ok_y)
        return [
            (ok_x & ok_y, corner(dx, dy, True, True, index)),
            (ok_x & no_y, corner(dx, dy, True, False, index)),
            (no_x & ok_y, corner(dx, dy, False, True, index)),
        ]

    for args in straights:

        @pl.when(inside(args[0], args[1]))
        def _():
            straight(*args).start()

    for index in range(4):
        for ok, copy in corner_cases(index):

            @pl.when(ok)
            def _():
                copy.start()

        dx, dy = CORNERS[index]

        @pl.when(jnp.logical_not(inside(dx, 0) | inside(0, dy)))
        def _():
            cor_in[index] = corpk[...]

    for slot, (dx, dy) in enumerate(((-1, 0), (1, 0), (0, -1), (0, 1))):

        @pl.when(jnp.logical_not(inside(dx, dy)))
        def _():
            if dx:
                reflect_rows(colpk, col_in.at[slot % 2], dx < 0, FLIP_X)
            else:
                reflect_rows(rowpk, row_in.at[slot % 2], dy < 0, FLIP_Y)

    for args in straights:

        @pl.when(inside(args[0], args[1]))
        def _():
            dx, dy, out_slot, _ = args
            back = straight(dx, dy, out_slot, out_slot)
            back.wait_send()
            back.wait_recv()

    for index in range(4):
        dx, dy = CORNERS[index]

        @pl.when(inside(dx, 0) | inside(0, dy))
        def _():
            copy = pltpu.make_async_remote_copy(
                src_ref=corpk,
                dst_ref=cor_in.at[index],
                send_sem=send_sem.at[4 + index],
                recv_sem=recv_sem.at[4 + index],
                device_id=peer(0, 0),
                device_id_type=MESH,
            )
            copy.wait_send()
            copy.wait_recv()

        @pl.when(jnp.logical_not(inside(0, dy)))
        def _():
            reflect_rows(cor_in.at[index], cor_in.at[index], dy < 0, FLIP_Y)

        @pl.when(jnp.logical_not(inside(dx, 0)))
        def _():
            block = cor_in[index]
            turned = block
            for j in range(max(DEPTHS)):
                if dx < 0:
                    moved = pltpu.roll(block, LANES - 1 - 2 * j, 1)
                    turned = jnp.where(lane == LANES - 1 - j, moved, turned)
                else:
                    moved = pltpu.roll(block, 2 * j + 1, 1)
                    turned = jnp.where(lane == j, moved, turned)
            cor_in[index] = turned * flip_signs((PACK, LANES), FLIP_X)

    low_w = before_mask((PACK, LANES))
    for b in range(side // LANES):
        cs = slice(b * LANES, (b + 1) * LANES)
        halo = jnp.where(low_w, col_in[0, :, cs], col_in[1, :, cs])
        halo = jnp.concatenate([halo, jnp.zeros((LANES - PACK, LANES), jnp.float32)], 0).T
        for field, seam in enumerate(SEAMS):
            ext[field, SUB + b * LANES : SUB + (b + 1) * LANES, width:ring] = pltpu.roll(
                halo, LANES - seam, 1
            )
    for field, (seam, depth) in enumerate(zip(SEAMS, DEPTHS)):
        north, south = slice(seam - depth, seam), slice(seam, seam + depth)
        top, end = slice(SUB - depth, SUB), slice(SUB + side, SUB + side + depth)
        ext[field, top, 0:width] = row_in[0, north, :]
        ext[field, end, 0:width] = row_in[1, south, :]
        east_lane = lax.broadcasted_iota(jnp.int32, (depth, LANES), 1) < LANES // 2
        ext[field, top, width:ring] = jnp.where(east_lane, cor_in[1, north], cor_in[0, north])
        ext[field, end, width:ring] = jnp.where(east_lane, cor_in[3, south], cor_in[2, south])

    def start_of(chunk):
        return chunk * SUB if isinstance(chunk, int) else pl.multiple_of(chunk * SUB, SUB)

    def beside(ref, lead, chunk, shift, columns=slice(None)):
        view = ref.at[lead + (pl.ds(start_of(chunk), 3 * SUB),)]
        return view[SUB + shift : 2 * SUB + shift, columns]

    def east_of(array):
        return pltpu.roll(array, ring - 1, 1)

    def west_of(array):
        return pltpu.roll(array, 1, 1)

    def spread(step, chunk, values):
        at = start_of(chunk)
        u, v, quarter, a, b = flux_parts(*values)
        for f in range(3):
            mix[step, f, pl.ds(at, SUB), :] = east_of(quarter[f] - a[f]) + west_of(quarter[f] + a[f])
            rise[step, f, pl.ds(at + SUB, SUB), :] = quarter[f] - b[f]
            fall[step, f, pl.ds(at + SUB, SUB), :] = quarter[f] + b[f]
        return u, v

    def gather(step, chunk, depth, slope_x, slope_y):
        at = start_of(chunk)
        pre = [
            mix[step, f, pl.ds(at, SUB), :]
            + beside(rise, (step, f), chunk, 1)
            + beside(fall, (step, f), chunk, -1)
            for f in range(3)
        ]
        return pre[0], pre[1] - depth * slope_x, pre[2] - depth * slope_y

    def drag_of(coef, pre):
        depth, east, south = pre
        square = east * east + south * south + SPEED_EPS
        inv_speed = lax.rsqrt(square)
        power = jnp.exp((-7.0 / 3.0) * jnp.log(depth))
        extra = coef * (square * inv_speed) * power
        return extra, inverse(1.0 + extra), inv_speed * inv_speed

    def stage_one(chunk):
        at = start_of(chunk)
        z = ext[3, pl.ds(at, SUB), :]
        scale = HALF_STEP * GRAVITY
        slopes[0, pl.ds(at, SUB), :] = scale * (east_of(z) - west_of(z))
        rise[0, 3, pl.ds(at + SUB, SUB), :] = scale * z
        spread(0, chunk, [ext[f, pl.ds(at, SUB), :] for f in range(3)])

    def stage_two(chunk):
        at = start_of(chunk)
        rows = pl.ds(at, SUB)
        depth, east, south = [ext[f, rows, :] for f in range(3)]
        slope_y = (
            beside(rise, (0, 3), chunk, 1) - beside(rise, (0, 3), chunk, -1)
        )
        slopes[1, rows, :] = slope_y
        pre = gather(0, chunk, depth, slopes[0, rows, :], slope_y)
        coef = ext[4, rows, :]
        is_wet = coef > 0
        extra, inv, _ = drag_of(coef, pre)
        now = [
            jnp.where(is_wet, pre[0], depth),
            jnp.where(is_wet, pre[1] * inv, east),
            jnp.where(is_wet, pre[2] * inv, south),
        ]
        damp[rows, :] = (extra * inv)[:, 0:width]
        for f in range(3):
            state[f, rows, :] = now[f]
        u, v = spread(1, chunk, now)
        vel[0, rows, :] = u[:, 0:width]
        vel[1, rows, :] = v[:, 0:width]

    def stage_three(chunk):
        at = start_of(chunk)
        rows = pl.ds(at, SUB)
        pre = gather(1, chunk, state[0, rows, :], slopes[0, rows, :], slopes[1, rows, :])
        coef = ext[4, rows, :]
        is_wet = coef > 0
        extra, inv, inv_square = drag_of(coef, pre)
        c_depth, c_east, c_south = [ext[5 + f, rows, :] for f in range(3)]
        t = -(c_east * pre[1] + c_south * pre[2]) * (inv * inv * extra)
        lam_rows = pl.ds(at + SUB, SUB)
        tq = t * inv_square
        lam[0, lam_rows, :] = jnp.where(is_wet, c_depth - (7.0 / 3.0) * t * inverse(pre[0]), 0.0)
        lam[1, lam_rows, :] = jnp.where(is_wet, c_east * inv + tq * pre[1], 0.0)
        lam[2, lam_rows, :] = jnp.where(is_wet, c_south * inv + tq * pre[2], 0.0)
        grad[rows, :] = t[:, 0:width]

    def stage_four(chunk):
        at = start_of(chunk)
        rows = pl.ds(at, SUB)
        mean, dx, dy = [], [], []
        for f in range(3):
            here = lam[f, pl.ds(at + SUB, SUB), :]
            east = east_of(here)[:, 0:width]
            west = west_of(here)[:, 0:width]
            south = beside(lam, (f,), chunk, 1, slice(0, width))
            north = beside(lam, (f,), chunk, -1, slice(0, width))
            if f:
                mean.append(0.25 * ((east + west) + (south + north)))
            dx.append(HALF_STEP * (east - west))
            dy.append(HALF_STEP * (south - north))
        u, v = vel[0, rows, :], vel[1, rows, :]
        cross = dx[2] + dy[1]
        a_east = mean[0] + dx[0] + 2.0 * u * dx[1] + v * cross
        a_south = mean[1] + dy[0] + 2.0 * v * dy[2] + u * cross
        total = grad[rows, :] - (
            a_east * state[1, rows, 0:width] + a_south * state[2, rows, 0:width]
        ) * damp[rows, :]
        is_wet = ext[4, rows, 0:width] > 0
        out = at - SUB if isinstance(chunk, int) else pl.multiple_of(at - SUB, SUB)
        grad_out[pl.ds(out, SUB), :] = jnp.where(is_wet, 2.0 * total, 0.0)

    stages = (
        (6, stage_four, 1, chunks - 1),
        (4, stage_three, 0, chunks),
        (2, stage_two, 0, chunks),
        (0, stage_one, 0, chunks),
    )

    def turn(i):
        for lag, stage, low, high in stages:
            if not isinstance(i, int) or low <= i - lag < high:
                stage(i - lag)

    first = 7
    for i in range(first):
        turn(i)

    def body(i, carry):
        turn(i)
        return carry

    lax.fori_loop(first, chunks, body, 0)
    for i in range(chunks, chunks + 6):
        turn(i)


def on_device(n_gx, n_gy, water_state, ground, log_rough, moment, second, wet_tiles, cotangent):
    side, width = ground.shape
    ring = width + LANES
    rows = side + 2 * SUB
    tall = rows + 2 * SUB
    f32 = jnp.float32
    in_hbm = pl.BlockSpec(memory_space=pltpu.HBM)
    gradient = pl.pallas_call(
        functools.partial(kernel, n_gx, n_gy),
        out_shape=jax.ShapeDtypeStruct((side, width), f32),
        in_specs=[in_hbm] * 5,
        out_specs=pl.BlockSpec(memory_space=pltpu.VMEM),
        scratch_shapes=[
            pltpu.SMEM(wet_tiles.shape, jnp.int32),
            pltpu.VMEM((8, rows, ring), f32),
            pltpu.VMEM((side, width), f32),
            pltpu.VMEM((PACK, side), f32),
            pltpu.VMEM((PACK, width), f32),
            pltpu.VMEM((PACK, LANES), f32),
            pltpu.VMEM((2, PACK, side), f32),
            pltpu.VMEM((2, PACK, width), f32),
            pltpu.VMEM((4, PACK, LANES), f32),
            pltpu.VMEM((2, rows, ring), f32),
            pltpu.VMEM((2, 3, rows, ring), f32),
            pltpu.VMEM((2, 4, tall, ring), f32),
            pltpu.VMEM((2, 3, tall, ring), f32),
            pltpu.VMEM((3, rows, ring), f32),
            pltpu.VMEM((rows, width), f32),
            pltpu.VMEM((2, rows, width), f32),
            pltpu.VMEM((3, tall, ring), f32),
            pltpu.VMEM((rows, width), f32),
            pltpu.SemaphoreType.DMA((5,)),
            pltpu.SemaphoreType.DMA((8,)),
            pltpu.SemaphoreType.DMA((8,)),
        ],
        compiler_params=pltpu.CompilerParams(
            collective_id=0, has_side_effects=True, vmem_limit_bytes=63 * 1024 * 1024
        ),
        name="flood_gradient",
    )(water_state, ground, log_rough, wet_tiles, cotangent)
    new_moment = BETA_ONE * moment + (1.0 - BETA_ONE) * gradient
    new_second = BETA_TWO * second + (1.0 - BETA_TWO) * gradient * gradient
    direction = jnp.arctan2(
        new_moment / (1.0 - BETA_ONE**UPDATES), jnp.sqrt(new_second / (1.0 - BETA_TWO**UPDATES))
    )
    new_rough = log_rough - LEARN_RATE * ATAN_SCALE * direction
    return (new_rough, new_moment, new_second)


def solution(mesh):
    field, plane = P(None, "gy", "gx"), P("gy", "gx")
    return jax.shard_map(
        functools.partial(on_device, mesh.shape["gx"], mesh.shape["gy"]),
        mesh=mesh,
        in_specs=(field, plane, plane, plane, plane, plane, field),
        out_specs=(plane, plane, plane),
        check_vma=False,
    )
```

```python
import functools

import jax
import jax.numpy as jnp
from jax import lax
from jax.experimental import pallas as pl
from jax.experimental.pallas import tpu as pltpu
from jax.sharding import PartitionSpec as P

UPDATES = 20
GRAVITY = 9.81
HALF_STEP = 0.05
GRAVITY_DT = 9.81
SPEED_EPS = 0.0001
BETA_ONE = 0.9
BETA_TWO = 0.999
LEARN_RATE = 0.05
ATAN_SCALE = 1.27

MESH = pl.DeviceIdType.MESH
DEPTHS = (3, 3, 3, 3, 2, 1, 1, 1)
SEAMS = (3, 9, 15, 21, 26, 29, 31, 33)
PACK = 40
FLIP_X = (1, 6)
FLIP_Y = (2, 7)
LANES = 128
SUB = 8
CORNERS = ((-1, -1), (1, -1), (-1, 1), (1, 1))


def flip_signs(shape, flipped):
    rows = lax.broadcasted_iota(jnp.int32, shape, 0)
    mask = jnp.zeros(shape, jnp.bool_)
    for field in flipped:
        seam, depth = SEAMS[field], DEPTHS[field]
        mask = mask | ((rows >= seam - depth) & (rows < seam + depth))
    return jnp.where(mask, -1.0, 1.0)


def reflect_rows(src, dst, low, flipped):
    for field, (seam, depth) in enumerate(zip(SEAMS, DEPTHS)):
        sign = -1.0 if field in flipped else 1.0
        for j in range(depth):
            a, b = (seam - 1 - j, seam + j) if low else (seam + j, seam - 1 - j)
            dst[a : a + 1, :] = sign * src[b : b + 1, :]


def inverse(x):
    guess = pl.reciprocal(x, approx=True)
    return guess * (2.0 - x * guess)


def flux_parts(depth, east, south):
    inv = inverse(depth)
    u, v = east * inv, south * inv
    press = (0.5 * GRAVITY) * depth * depth
    qh, qe, qs = 0.25 * depth, 0.25 * east, 0.25 * south
    a0 = HALF_STEP * east
    a1 = HALF_STEP * (east * u + press)
    a2 = HALF_STEP * (east * v)
    b0 = HALF_STEP * south
    b2 = HALF_STEP * (south * v + press)
    return u, v, (qh, qe, qs), (a0, a1, a2), (b0, a2, b2)


def kernel(
    n_gx,
    n_gy,
    water,
    ground,
    rough,
    wet_tiles,
    cot,
    grad_out,
    wet,
    ext,
    rough_v,
    colpk,
    rowpk,
    corpk,
    col_in,
    row_in,
    cor_in,
    slopes,
    mix,
    rise,
    fall,
    state,
    damp,
    vel,
    lam,
    grad,
    load_sem,
    send_sem,
    recv_sem,
):
    side = rough.shape[0]
    width = rough.shape[1]
    tile_rows, tile_cols = wet.shape
    tile_h, tile_w = side // tile_rows, width // tile_cols
    ring = width + LANES
    chunks = side // SUB + 2
    gx = lax.axis_index("gx")
    gy = lax.axis_index("gy")

    def inside(dx, dy):
        checks = []
        if dx < 0:
            checks.append(gx > 0)
        if dx > 0:
            checks.append(gx < n_gx - 1)
        if dy < 0:
            checks.append(gy > 0)
        if dy > 0:
            checks.append(gy < n_gy - 1)
        return functools.reduce(jnp.logical_and, checks)

    def peer(dx, dy):
        return {"gx": gx + dx, "gy": gy + dy}

    loads = [
        pltpu.make_async_copy(water, ext.at[0:3, SUB : SUB + side, 0:width], load_sem.at[0]),
        pltpu.make_async_copy(rough, rough_v, load_sem.at[1]),
        pltpu.make_async_copy(ground, ext.at[3, SUB : SUB + side, 0:width], load_sem.at[2]),
        pltpu.make_async_copy(cot, ext.at[5:8, SUB : SUB + side, 0:width], load_sem.at[3]),
        pltpu.make_async_copy(wet_tiles, wet, load_sem.at[4]),
    ]
    for load in loads:
        load.start()

    barrier = pltpu.get_barrier_semaphore()
    around = [(dx, dy) for dx in (-1, 0, 1) for dy in (-1, 0, 1) if (dx, dy) != (0, 0)]
    count = jnp.int32(0)
    for dx, dy in around:
        ok = inside(dx, dy)

        @pl.when(ok)
        def _():
            pl.semaphore_signal(barrier, inc=1, device_id=peer(dx, dy), device_id_type=MESH)

        count = count + ok.astype(jnp.int32)

    for load in loads:
        load.wait()
    for i in range(tile_rows):
        for j in range(tile_cols):
            rs, cs = slice(i * tile_h, (i + 1) * tile_h), slice(j * tile_w, (j + 1) * tile_w)
            coef = GRAVITY_DT * jnp.exp(2.0 * rough_v[rs, cs])
            ext[4, SUB + i * tile_h : SUB + (i + 1) * tile_h, cs] = jnp.where(
                wet[i, j] > 0, coef, -1.0
            )

    for field, (seam, depth) in enumerate(zip(SEAMS, DEPTHS)):
        rowpk[seam - depth : seam, :] = ext[field, SUB + side - depth : SUB + side, 0:width]
        rowpk[seam : seam + depth, :] = ext[field, SUB : SUB + depth, 0:width]
    lane = lax.broadcasted_iota(jnp.int32, (PACK, LANES), 1)
    corpk[...] = jnp.where(lane < LANES // 2, rowpk[:, 0:LANES], rowpk[:, width - LANES : width])
    lane_b = lax.broadcasted_iota(jnp.int32, (LANES, LANES), 1)
    for b in range(side // LANES):
        packed = jnp.zeros((LANES, LANES), jnp.float32)
        rs = slice(SUB + b * LANES, SUB + (b + 1) * LANES)
        for field, (seam, depth) in enumerate(zip(SEAMS, DEPTHS)):
            both = jnp.where(
                lane_b < LANES // 2, ext[field, rs, 0:LANES], ext[field, rs, width - LANES : width]
            )
            both = pltpu.roll(both, seam, 1)
            packed = jnp.where((lane_b >= seam - depth) & (lane_b < seam + depth), both, packed)
        colpk[:, b * LANES : (b + 1) * LANES] = packed.T[0:PACK]

    pl.semaphore_wait(barrier, count)

    def straight(dx, dy, out_slot, in_slot):
        src, dst = (colpk, col_in) if dx else (rowpk, row_in)
        return pltpu.make_async_remote_copy(
            src_ref=src,
            dst_ref=dst.at[in_slot % 2],
            send_sem=send_sem.at[out_slot],
            recv_sem=recv_sem.at[in_slot],
            device_id=peer(dx, dy),
            device_id_type=MESH,
        )

    straights = [(-1, 0, 0, 1), (1, 0, 1, 0), (0, -1, 2, 3), (0, 1, 3, 2)]

    def corner(dx, dy, in_x, in_y, index):
        slot = CORNERS.index((-dx if in_x else dx, -dy if in_y else dy))
        return pltpu.make_async_remote_copy(
            src_ref=corpk,
            dst_ref=cor_in.at[slot],
            send_sem=send_sem.at[4 + index],
            recv_sem=recv_sem.at[4 + slot],
            device_id=peer(dx if in_x else 0, dy if in_y else 0),
            device_id_type=MESH,
        )

    def corner_cases(index):
        dx, dy = CORNERS[index]
        ok_x, ok_y = inside(dx, 0), inside(0, dy)
        no_x, no_y = jnp.logical_not(ok_x), jnp.logical_not(ok_y)
        return [
            (ok_x & ok_y, corner(dx, dy, True, True, index)),
            (ok_x & no_y, corner(dx, dy, True, False, index)),
            (no_x & ok_y, corner(dx, dy, False, True, index)),
        ]

    for args in straights:

        @pl.when(inside(args[0], args[1]))
        def _():
            straight(*args).start()

    for index in range(4):
        for ok, copy in corner_cases(index):

            @pl.when(ok)
            def _():
                copy.start()

        dx, dy = CORNERS[index]

        @pl.when(jnp.logical_not(inside(dx, 0) | inside(0, dy)))
        def _():
            cor_in[index] = corpk[...]

    for slot, (dx, dy) in enumerate(((-1, 0), (1, 0), (0, -1), (0, 1))):

        @pl.when(jnp.logical_not(inside(dx, dy)))
        def _():
            if dx:
                reflect_rows(colpk, col_in.at[slot % 2], dx < 0, FLIP_X)
            else:
                reflect_rows(rowpk, row_in.at[slot % 2], dy < 0, FLIP_Y)

    def beside(ref, lead, at, rows, zone, shift):
        view = ref.at[lead + (pl.ds(at, rows + 2 * SUB),)]
        return view[SUB + shift : SUB + rows + shift, zone]

    def east_of(array):
        return pltpu.roll(array, array.shape[1] - 1, 1)

    def west_of(array):
        return pltpu.roll(array, 1, 1)

    def spread(step, at, rows, zone, values):
        here, inner = pl.ds(at, rows), pl.ds(at + SUB, rows)
        u, v, quarter, a, b = flux_parts(*values)
        for f in range(3):
            mix[step, f, here, zone] = east_of(quarter[f] - a[f]) + west_of(quarter[f] + a[f])
            rise[step, f, inner, zone] = quarter[f] - b[f]
            fall[step, f, inner, zone] = quarter[f] + b[f]
        return u, v

    def gather(step, at, rows, zone, depth, slope_x, slope_y):
        pre = [
            mix[step, f, pl.ds(at, rows), zone]
            + beside(rise, (step, f), at, rows, zone, 1)
            + beside(fall, (step, f), at, rows, zone, -1)
            for f in range(3)
        ]
        return pre[0], pre[1] - depth * slope_x, pre[2] - depth * slope_y

    def drag_of(coef, pre):
        depth, east, south = pre
        square = east * east + south * south + SPEED_EPS
        inv_speed = lax.rsqrt(square)
        power = jnp.exp((-7.0 / 3.0) * jnp.log(depth))
        extra = coef * (square * inv_speed) * power
        return extra, inverse(1.0 + extra), inv_speed * inv_speed

    def stage_one(at, rows, zone):
        here = pl.ds(at, rows)
        z = (HALF_STEP * GRAVITY) * ext[3, here, zone]
        slopes[0, here, zone] = east_of(z) - west_of(z)
        rise[0, 3, pl.ds(at + SUB, rows), zone] = z
        spread(0, at, rows, zone, [ext[f, here, zone] for f in range(3)])

    def stage_two(at, rows, zone):
        here = pl.ds(at, rows)
        depth, east, south = [ext[f, here, zone] for f in range(3)]
        slope_y = beside(rise, (0, 3), at, rows, zone, 1) - beside(rise, (0, 3), at, rows, zone, -1)
        slopes[1, here, zone] = slope_y
        pre = gather(0, at, rows, zone, depth, slopes[0, here, zone], slope_y)
        coef = ext[4, here, zone]
        is_wet = coef > 0
        extra, inv, _ = drag_of(coef, pre)
        now = [
            jnp.where(is_wet, pre[0], depth),
            jnp.where(is_wet, pre[1] * inv, east),
            jnp.where(is_wet, pre[2] * inv, south),
        ]
        damp[here, zone] = extra * inv
        for f in range(3):
            state[f, here, zone] = now[f]
        u, v = spread(1, at, rows, zone, now)
        vel[0, here, zone] = u
        vel[1, here, zone] = v

    def stage_three(at, rows, zone):
        here = pl.ds(at, rows)
        pre = gather(1, at, rows, zone, state[0, here, zone], slopes[0, here, zone], slopes[1, here, zone])
        coef = ext[4, here, zone]
        is_wet = coef > 0
        extra, inv, inv_square = drag_of(coef, pre)
        c_depth, c_east, c_south = [ext[5 + f, here, zone] for f in range(3)]
        t = -(c_east * pre[1] + c_south * pre[2]) * (inv * inv * extra)
        inner = pl.ds(at + SUB, rows)
        tq = t * inv_square
        lam[0, inner, zone] = jnp.where(is_wet, c_depth - (7.0 / 3.0) * t * inverse(pre[0]), 0.0)
        lam[1, inner, zone] = jnp.where(is_wet, c_east * inv + tq * pre[1], 0.0)
        lam[2, inner, zone] = jnp.where(is_wet, c_south * inv + tq * pre[2], 0.0)
        grad[here, zone] = t

    def stage_four(at, rows, zone):
        here = pl.ds(at, rows)
        mean, dx, dy = [], [], []
        for f in range(3):
            mid = lam[f, pl.ds(at + SUB, rows), zone]
            east, west = east_of(mid), west_of(mid)
            south = beside(lam, (f,), at, rows, zone, 1)
            north = beside(lam, (f,), at, rows, zone, -1)
            if f:
                mean.append(0.25 * ((east + west) + (south + north)))
            dx.append(HALF_STEP * (east - west))
            dy.append(HALF_STEP * (south - north))
        u, v = vel[0, here, zone], vel[1, here, zone]
        cross = dx[2] + dy[1]
        a_east = mean[0] + dx[0] + 2.0 * u * dx[1] + v * cross
        a_south = mean[1] + dy[0] + 2.0 * v * dy[2] + u * cross
        total = grad[here, zone] - (
            a_east * state[1, here, zone] + a_south * state[2, here, zone]
        ) * damp[here, zone]
        result = jnp.where(ext[4, here, zone] > 0, 2.0 * total, 0.0)
        if zone is seam_zone:
            grad[here, zone] = result
        else:
            out = at - SUB
            out = out if isinstance(out, int) else pl.multiple_of(out, SUB)
            grad_out[pl.ds(out, rows), :] = result

    def run(stages, rows, zone):
        def turn(i):
            for lag, stage, low, high in stages:
                if not isinstance(i, int):
                    stage(pl.multiple_of((i - lag) * rows, SUB), rows, zone)
                elif low <= i - lag < high:
                    stage((i - lag) * rows, rows, zone)

        def body(i, carry):
            turn(i)
            return carry

        begin = min(lag + low for lag, _, low, _ in stages)
        full = max(lag + low for lag, _, low, _ in stages)
        drain = min(lag + high for lag, _, _, high in stages)
        end = max(lag + high for lag, _, _, high in stages)
        for i in range(begin, full):
            turn(i)
        lax.fori_loop(full, drain, body, 0)
        for i in range(drain, end):
            turn(i)

    main_zone, seam_zone = slice(0, width), slice(width, ring)
    half, quart = LANES // 2, LANES // 4
    for b in range(side // LANES):
        rs = slice(SUB + b * LANES, SUB + (b + 1) * LANES)
        for field in range(8):
            ext[field, rs, seam_zone] = jnp.where(
                lane_b < half,
                pltpu.roll(ext[field, rs, width - LANES : width], quart, 1),
                pltpu.roll(ext[field, rs, 0:LANES], LANES - quart, 1),
            )
    run(
        (
            (6, stage_four, 4, chunks - 4),
            (4, stage_three, 3, chunks - 3),
            (2, stage_two, 2, chunks - 2),
            (0, stage_one, 1, chunks - 1),
        ),
        SUB,
        main_zone,
    )

    for args in straights:

        @pl.when(inside(args[0], args[1]))
        def _():
            dx, dy, out_slot, _ = args
            back = straight(dx, dy, out_slot, out_slot)
            back.wait_send()
            back.wait_recv()

    for index in range(4):
        dx, dy = CORNERS[index]

        @pl.when(inside(dx, 0) | inside(0, dy))
        def _():
            copy = pltpu.make_async_remote_copy(
                src_ref=corpk,
                dst_ref=cor_in.at[index],
                send_sem=send_sem.at[4 + index],
                recv_sem=recv_sem.at[4 + index],
                device_id=peer(0, 0),
                device_id_type=MESH,
            )
            copy.wait_send()
            copy.wait_recv()

        @pl.when(jnp.logical_not(inside(0, dy)))
        def _():
            reflect_rows(cor_in.at[index], cor_in.at[index], dy < 0, FLIP_Y)

        @pl.when(jnp.logical_not(inside(dx, 0)))
        def _():
            block = cor_in[index]
            turned = block
            for j in range(max(DEPTHS)):
                if dx < 0:
                    moved = pltpu.roll(block, LANES - 1 - 2 * j, 1)
                    turned = jnp.where(lane == LANES - 1 - j, moved, turned)
                else:
                    moved = pltpu.roll(block, 2 * j + 1, 1)
                    turned = jnp.where(lane == j, moved, turned)
            cor_in[index] = turned * flip_signs((PACK, LANES), FLIP_X)

    gap = jnp.zeros((half - PACK, LANES), jnp.float32)
    for b in range(side // LANES):
        cs = slice(b * LANES, (b + 1) * LANES)
        rs = slice(SUB + b * LANES, SUB + (b + 1) * LANES)
        halo = jnp.concatenate([col_in[1, :, cs], gap, col_in[0, :, cs], gap], 0).T
        for field, seam in enumerate(SEAMS):
            moved = pltpu.roll(halo, (LANES + quart - seam) % LANES, 1)
            ext[field, rs, seam_zone] = jnp.where(
                (lane_b >= quart) & (lane_b < LANES - quart), moved, ext[field, rs, seam_zone]
            )
    for i in range(2):
        first, last = row_in[i, :, 0:LANES], row_in[i, :, width - LANES : width]
        west, east = cor_in[2 * i], cor_in[2 * i + 1]
        cor_in[2 * i] = jnp.where(
            lane < half,
            pltpu.roll(jnp.where(lane < half, east, last), quart, 1),
            pltpu.roll(jnp.where(lane < half, first, west), LANES - quart, 1),
        )
    for field, (seam, depth) in enumerate(zip(SEAMS, DEPTHS)):
        north, south = slice(seam - depth, seam), slice(seam, seam + depth)
        top, end = slice(SUB - depth, SUB), slice(SUB + side, SUB + side + depth)
        ext[field, top, main_zone] = row_in[0, north, :]
        ext[field, end, main_zone] = row_in[1, south, :]
        ext[field, top, seam_zone] = cor_in[0, north, :]
        ext[field, end, seam_zone] = cor_in[2, south, :]

    for depth, stage in enumerate((stage_one, stage_two, stage_three, stage_four)):
        low = 1 if stage is stage_four else 0
        for k in range(depth + 1 - low):
            stage((k + low) * SUB, SUB, main_zone)
            stage((chunks - 1 - k - low) * SUB, SUB, main_zone)
    tall = chunks // 2
    run(
        (
            (6, stage_four, 0, tall),
            (4, stage_three, 0, tall),
            (2, stage_two, 0, tall),
            (0, stage_one, 0, tall),
        ),
        2 * SUB,
        seam_zone,
    )
    reach = max(DEPTHS)
    for b in range(side // LANES):
        rs = slice(b * LANES, (b + 1) * LANES)
        found = grad[SUB + b * LANES : SUB + (b + 1) * LANES, seam_zone]
        grad_out[rs, 0:LANES] = jnp.where(
            lane_b < reach, pltpu.roll(found, quart, 1), grad_out[rs, 0:LANES]
        )
        grad_out[rs, width - LANES : width] = jnp.where(
            lane_b >= LANES - reach,
            pltpu.roll(found, LANES - quart, 1),
            grad_out[rs, width - LANES : width],
        )


def on_device(n_gx, n_gy, water_state, ground, log_rough, moment, second, wet_tiles, cotangent):
    side, width = ground.shape
    ring = width + LANES
    rows = side + 2 * SUB
    tall = rows + 2 * SUB
    f32 = jnp.float32
    in_hbm = pl.BlockSpec(memory_space=pltpu.HBM)
    gradient = pl.pallas_call(
        functools.partial(kernel, n_gx, n_gy),
        out_shape=jax.ShapeDtypeStruct((side, width), f32),
        in_specs=[in_hbm] * 5,
        out_specs=pl.BlockSpec(memory_space=pltpu.VMEM),
        scratch_shapes=[
            pltpu.SMEM(wet_tiles.shape, jnp.int32),
            pltpu.VMEM((8, rows, ring), f32),
            pltpu.VMEM((side, width), f32),
            pltpu.VMEM((PACK, side), f32),
            pltpu.VMEM((PACK, width), f32),
            pltpu.VMEM((PACK, LANES), f32),
            pltpu.VMEM((2, PACK, side), f32),
            pltpu.VMEM((2, PACK, width), f32),
            pltpu.VMEM((4, PACK, LANES), f32),
            pltpu.VMEM((2, rows, ring), f32),
            pltpu.VMEM((2, 3, rows, ring), f32),
            pltpu.VMEM((2, 4, tall, ring), f32),
            pltpu.VMEM((2, 3, tall, ring), f32),
            pltpu.VMEM((3, rows, ring), f32),
            pltpu.VMEM((rows, ring), f32),
            pltpu.VMEM((2, rows, ring), f32),
            pltpu.VMEM((3, tall, ring), f32),
            pltpu.VMEM((rows, ring), f32),
            pltpu.SemaphoreType.DMA((5,)),
            pltpu.SemaphoreType.DMA((8,)),
            pltpu.SemaphoreType.DMA((8,)),
        ],
        compiler_params=pltpu.CompilerParams(
            collective_id=0, has_side_effects=True, vmem_limit_bytes=63 * 1024 * 1024
        ),
        name="flood_gradient",
    )(water_state, ground, log_rough, wet_tiles, cotangent)
    new_moment = BETA_ONE * moment + (1.0 - BETA_ONE) * gradient
    new_second = BETA_TWO * second + (1.0 - BETA_TWO) * gradient * gradient
    direction = jnp.arctan2(
        new_moment / (1.0 - BETA_ONE**UPDATES), jnp.sqrt(new_second / (1.0 - BETA_TWO**UPDATES))
    )
    new_rough = log_rough - LEARN_RATE * ATAN_SCALE * direction
    return (new_rough, new_moment, new_second)


def solution(mesh):
    field, plane = P(None, "gy", "gx"), P("gy", "gx")
    return jax.shard_map(
        functools.partial(on_device, mesh.shape["gx"], mesh.shape["gy"]),
        mesh=mesh,
        in_specs=(field, plane, plane, plane, plane, plane, field),
        out_specs=(plane, plane, plane),
        check_vma=False,
    )
```

```python
import functools

import jax
import jax.numpy as jnp
from jax import lax
from jax.experimental import pallas as pl
from jax.experimental.pallas import tpu as pltpu
from jax.sharding import PartitionSpec as P

UPDATES = 20
GRAVITY = 9.81
HALF_STEP = 0.05
GRAVITY_DT = 9.81
SPEED_EPS = 0.0001
BETA_ONE = 0.9
BETA_TWO = 0.999
LEARN_RATE = 0.05
ATAN_SCALE = 1.27

MESH = pl.DeviceIdType.MESH
DEPTHS = (3, 3, 3, 3, 2, 1, 1, 1)
SEAMS = (3, 9, 15, 21, 26, 29, 31, 33)
PACK = 40
LIMIT = 62
FLIP_X = (1, 6)
FLIP_Y = (2, 7)
LANES = 128
SUB = 8
CORNERS = ((-1, -1), (1, -1), (-1, 1), (1, 1))


def flip_signs(shape, flipped):
    rows = lax.broadcasted_iota(jnp.int32, shape, 0)
    mask = jnp.zeros(shape, jnp.bool_)
    for field in flipped:
        seam, depth = SEAMS[field], DEPTHS[field]
        mask = mask | ((rows >= seam - depth) & (rows < seam + depth))
    return jnp.where(mask, -1.0, 1.0)


def reflect_rows(src, dst, low, flipped):
    for field, (seam, depth) in enumerate(zip(SEAMS, DEPTHS)):
        sign = -1.0 if field in flipped else 1.0
        for j in range(depth):
            a, b = (seam - 1 - j, seam + j) if low else (seam + j, seam - 1 - j)
            dst[a : a + 1, :] = sign * src[b : b + 1, :]


def inverse(x):
    guess = pl.reciprocal(x, approx=True)
    return guess * (2.0 - x * guess)


def flux_parts(depth, east, south):
    inv = inverse(depth)
    u, v = east * inv, south * inv
    press = (0.5 * GRAVITY) * depth * depth
    qh, qe, qs = 0.25 * depth, 0.25 * east, 0.25 * south
    a0 = HALF_STEP * east
    a1 = HALF_STEP * (east * u + press)
    a2 = HALF_STEP * (east * v)
    b0 = HALF_STEP * south
    b2 = HALF_STEP * (south * v + press)
    return u, v, (qh, qe, qs), (a0, a1, a2), (b0, a2, b2)


def kernel(
    n_gx,
    n_gy,
    water,
    ground,
    rough,
    wet_tiles,
    cot,
    grad_out,
    wet,
    ext,
    rough_v,
    colpk,
    rowpk,
    corpk,
    col_in,
    row_in,
    cor_in,
    slopes,
    mix,
    rise,
    fall,
    state,
    damp,
    vel,
    lam,
    grad,
    load_sem,
    send_sem,
    recv_sem,
):
    side = rough.shape[0]
    width = rough.shape[1]
    tile_rows, tile_cols = wet.shape
    tile_h, tile_w = side // tile_rows, width // tile_cols
    ring = width + LANES
    chunks = side // SUB + 2
    gx = lax.axis_index("gx")
    gy = lax.axis_index("gy")

    def inside(dx, dy):
        checks = []
        if dx < 0:
            checks.append(gx > 0)
        if dx > 0:
            checks.append(gx < n_gx - 1)
        if dy < 0:
            checks.append(gy > 0)
        if dy > 0:
            checks.append(gy < n_gy - 1)
        return functools.reduce(jnp.logical_and, checks)

    def peer(dx, dy):
        return {"gx": gx + dx, "gy": gy + dy}

    loads = [
        pltpu.make_async_copy(water, ext.at[0:3, SUB : SUB + side, 0:width], load_sem.at[0]),
        pltpu.make_async_copy(rough, rough_v, load_sem.at[1]),
        pltpu.make_async_copy(ground, ext.at[3, SUB : SUB + side, 0:width], load_sem.at[2]),
        pltpu.make_async_copy(cot, ext.at[5:8, SUB : SUB + side, 0:width], load_sem.at[3]),
        pltpu.make_async_copy(wet_tiles, wet, load_sem.at[4]),
    ]
    for load in loads:
        load.start()

    barrier = pltpu.get_barrier_semaphore()
    around = [(dx, dy) for dx in (-1, 0, 1) for dy in (-1, 0, 1) if (dx, dy) != (0, 0)]
    count = jnp.int32(0)
    for dx, dy in around:
        ok = inside(dx, dy)

        @pl.when(ok)
        def _():
            pl.semaphore_signal(barrier, inc=1, device_id=peer(dx, dy), device_id_type=MESH)

        count = count + ok.astype(jnp.int32)

    for load in loads:
        load.wait()
    for i in range(tile_rows):
        for j in range(tile_cols):
            rs, cs = slice(i * tile_h, (i + 1) * tile_h), slice(j * tile_w, (j + 1) * tile_w)
            coef = GRAVITY_DT * jnp.exp(2.0 * rough_v[rs, cs])
            ext[4, SUB + i * tile_h : SUB + (i + 1) * tile_h, cs] = jnp.where(
                wet[i, j] > 0, coef, -1.0
            )

    lane_b = lax.broadcasted_iota(jnp.int32, (LANES, LANES), 1)
    for b in range(side // LANES):
        packed = jnp.zeros((LANES, LANES), jnp.float32)
        rs = slice(SUB + b * LANES, SUB + (b + 1) * LANES)
        for field, (seam, depth) in enumerate(zip(SEAMS, DEPTHS)):
            both = jnp.where(
                lane_b < LANES // 2, ext[field, rs, 0:LANES], ext[field, rs, width - LANES : width]
            )
            both = pltpu.roll(both, seam, 1)
            packed = jnp.where((lane_b >= seam - depth) & (lane_b < seam + depth), both, packed)
        colpk[:, b * LANES : (b + 1) * LANES] = packed.T[0:PACK]

    pl.semaphore_wait(barrier, count)

    def straight(dx, dy, out_slot, in_slot):
        src, dst = (colpk, col_in) if dx else (rowpk, row_in)
        return pltpu.make_async_remote_copy(
            src_ref=src,
            dst_ref=dst.at[in_slot % 2],
            send_sem=send_sem.at[out_slot],
            recv_sem=recv_sem.at[in_slot],
            device_id=peer(dx, dy),
            device_id_type=MESH,
        )

    straights = [(-1, 0, 0, 1), (1, 0, 1, 0), (0, -1, 2, 3), (0, 1, 3, 2)]

    def corner(dx, dy, in_x, in_y, index):
        slot = CORNERS.index((-dx if in_x else dx, -dy if in_y else dy))
        return pltpu.make_async_remote_copy(
            src_ref=corpk,
            dst_ref=cor_in.at[slot],
            send_sem=send_sem.at[4 + index],
            recv_sem=recv_sem.at[4 + slot],
            device_id=peer(dx if in_x else 0, dy if in_y else 0),
            device_id_type=MESH,
        )

    def corner_cases(index):
        dx, dy = CORNERS[index]
        ok_x, ok_y = inside(dx, 0), inside(0, dy)
        no_x, no_y = jnp.logical_not(ok_x), jnp.logical_not(ok_y)
        return [
            (ok_x & ok_y, corner(dx, dy, True, True, index)),
            (ok_x & no_y, corner(dx, dy, True, False, index)),
            (no_x & ok_y, corner(dx, dy, False, True, index)),
        ]

    for args in straights[:2]:

        @pl.when(inside(args[0], args[1]))
        def _():
            straight(*args).start()

    for field, (seam, depth) in enumerate(zip(SEAMS, DEPTHS)):
        rowpk[seam - depth : seam, :] = ext[field, SUB + side - depth : SUB + side, 0:width]
        rowpk[seam : seam + depth, :] = ext[field, SUB : SUB + depth, 0:width]
    lane = lax.broadcasted_iota(jnp.int32, (PACK, LANES), 1)
    corpk[...] = jnp.where(lane < LANES // 2, rowpk[:, 0:LANES], rowpk[:, width - LANES : width])
    for args in straights[2:]:

        @pl.when(inside(args[0], args[1]))
        def _():
            straight(*args).start()

    for index in range(4):
        for ok, copy in corner_cases(index):

            @pl.when(ok)
            def _():
                copy.start()

        dx, dy = CORNERS[index]

        @pl.when(jnp.logical_not(inside(dx, 0) | inside(0, dy)))
        def _():
            cor_in[index] = corpk[...]

    for slot, (dx, dy) in enumerate(((-1, 0), (1, 0), (0, -1), (0, 1))):

        @pl.when(jnp.logical_not(inside(dx, dy)))
        def _():
            if dx:
                reflect_rows(colpk, col_in.at[slot % 2], dx < 0, FLIP_X)
            else:
                reflect_rows(rowpk, row_in.at[slot % 2], dy < 0, FLIP_Y)

    def beside(ref, lead, at, rows, zone, shift):
        view = ref.at[lead + (pl.ds(at, rows + 2 * SUB),)]
        return view[SUB + shift : SUB + rows + shift, zone]

    def east_of(array):
        return pltpu.roll(array, array.shape[1] - 1, 1)

    def west_of(array):
        return pltpu.roll(array, 1, 1)

    def spread(step, at, rows, zone, values):
        here, inner = pl.ds(at, rows), pl.ds(at + SUB, rows)
        u, v, quarter, a, b = flux_parts(*values)
        for f in range(3):
            mix[step, f, here, zone] = east_of(quarter[f] - a[f]) + west_of(quarter[f] + a[f])
            rise[step, f, inner, zone] = quarter[f] - b[f]
            fall[step, f, inner, zone] = quarter[f] + b[f]
        return u, v

    def gather(step, at, rows, zone, depth, slope_x, slope_y):
        pre = [
            mix[step, f, pl.ds(at, rows), zone]
            + beside(rise, (step, f), at, rows, zone, 1)
            + beside(fall, (step, f), at, rows, zone, -1)
            for f in range(3)
        ]
        return pre[0], pre[1] - depth * slope_x, pre[2] - depth * slope_y

    def drag_of(coef, pre):
        depth, east, south = pre
        square = east * east + south * south + SPEED_EPS
        inv_speed = lax.rsqrt(square)
        power = jnp.exp((-7.0 / 3.0) * jnp.log(depth))
        extra = coef * (square * inv_speed) * power
        return extra, inverse(1.0 + extra), inv_speed * inv_speed

    def stage_one(at, rows, zone):
        here = pl.ds(at, rows)
        z = (HALF_STEP * GRAVITY) * ext[3, here, zone]
        slopes[0, here, zone] = east_of(z) - west_of(z)
        rise[0, 3, pl.ds(at + SUB, rows), zone] = z
        spread(0, at, rows, zone, [ext[f, here, zone] for f in range(3)])

    def stage_two(at, rows, zone):
        here = pl.ds(at, rows)
        depth, east, south = [ext[f, here, zone] for f in range(3)]
        slope_y = beside(rise, (0, 3), at, rows, zone, 1) - beside(rise, (0, 3), at, rows, zone, -1)
        slopes[1, here, zone] = slope_y
        pre = gather(0, at, rows, zone, depth, slopes[0, here, zone], slope_y)
        coef = ext[4, here, zone]
        is_wet = coef > 0
        extra, inv, _ = drag_of(coef, pre)
        now = [
            jnp.where(is_wet, pre[0], depth),
            jnp.where(is_wet, pre[1] * inv, east),
            jnp.where(is_wet, pre[2] * inv, south),
        ]
        damp[here, zone] = extra * inv
        for f in range(3):
            state[f, here, zone] = now[f]
        u, v = spread(1, at, rows, zone, now)
        vel[0, here, zone] = u
        vel[1, here, zone] = v

    def stage_three(at, rows, zone):
        here = pl.ds(at, rows)
        pre = gather(1, at, rows, zone, state[0, here, zone], slopes[0, here, zone], slopes[1, here, zone])
        coef = ext[4, here, zone]
        is_wet = coef > 0
        extra, inv, inv_square = drag_of(coef, pre)
        c_depth, c_east, c_south = [ext[5 + f, here, zone] for f in range(3)]
        t = -(c_east * pre[1] + c_south * pre[2]) * (inv * inv * extra)
        inner = pl.ds(at + SUB, rows)
        tq = t * inv_square
        lam[0, inner, zone] = jnp.where(is_wet, c_depth - (7.0 / 3.0) * t * inverse(pre[0]), 0.0)
        lam[1, inner, zone] = jnp.where(is_wet, c_east * inv + tq * pre[1], 0.0)
        lam[2, inner, zone] = jnp.where(is_wet, c_south * inv + tq * pre[2], 0.0)
        grad[here, zone] = t

    def stage_four(at, rows, zone):
        here = pl.ds(at, rows)
        mean, dx, dy = [], [], []
        for f in range(3):
            mid = lam[f, pl.ds(at + SUB, rows), zone]
            east, west = east_of(mid), west_of(mid)
            south = beside(lam, (f,), at, rows, zone, 1)
            north = beside(lam, (f,), at, rows, zone, -1)
            if f:
                mean.append(0.25 * ((east + west) + (south + north)))
            dx.append(HALF_STEP * (east - west))
            dy.append(HALF_STEP * (south - north))
        u, v = vel[0, here, zone], vel[1, here, zone]
        cross = dx[2] + dy[1]
        a_east = mean[0] + dx[0] + 2.0 * u * dx[1] + v * cross
        a_south = mean[1] + dy[0] + 2.0 * v * dy[2] + u * cross
        total = grad[here, zone] - (
            a_east * state[1, here, zone] + a_south * state[2, here, zone]
        ) * damp[here, zone]
        result = jnp.where(ext[4, here, zone] > 0, 2.0 * total, 0.0)
        if zone is seam_zone:
            grad[here, zone] = result
        else:
            out = at - SUB
            out = out if isinstance(out, int) else pl.multiple_of(out, SUB)
            grad_out[pl.ds(out, rows), :] = result

    def run(stages, rows, zone):
        def turn(i):
            for lag, stage, low, high in stages:
                if not isinstance(i, int):
                    stage(pl.multiple_of((i - lag) * rows, SUB), rows, zone)
                elif low <= i - lag < high:
                    stage((i - lag) * rows, rows, zone)

        def body(i, carry):
            turn(i)
            return carry

        begin = min(lag + low for lag, _, low, _ in stages)
        full = max(lag + low for lag, _, low, _ in stages)
        drain = min(lag + high for lag, _, _, high in stages)
        end = max(lag + high for lag, _, _, high in stages)
        for i in range(begin, full):
            turn(i)
        lax.fori_loop(full, drain, body, 0)
        for i in range(drain, end):
            turn(i)

    main_zone, seam_zone = slice(0, width), slice(width, ring)
    half, quart = LANES // 2, LANES // 4
    for b in range(side // LANES):
        rs = slice(SUB + b * LANES, SUB + (b + 1) * LANES)
        for field in range(8):
            ext[field, rs, seam_zone] = jnp.where(
                lane_b < half,
                pltpu.roll(ext[field, rs, width - LANES : width], quart, 1),
                pltpu.roll(ext[field, rs, 0:LANES], LANES - quart, 1),
            )
    run(
        (
            (6, stage_four, 4, chunks - 4),
            (4, stage_three, 3, chunks - 3),
            (2, stage_two, 2, chunks - 2),
            (0, stage_one, 1, chunks - 1),
        ),
        SUB,
        main_zone,
    )

    for args in straights:

        @pl.when(inside(args[0], args[1]))
        def _():
            dx, dy, out_slot, _ = args
            back = straight(dx, dy, out_slot, out_slot)
            back.wait_send()
            back.wait_recv()

    for index in range(4):
        dx, dy = CORNERS[index]

        @pl.when(inside(dx, 0) | inside(0, dy))
        def _():
            copy = pltpu.make_async_remote_copy(
                src_ref=corpk,
                dst_ref=cor_in.at[index],
                send_sem=send_sem.at[4 + index],
                recv_sem=recv_sem.at[4 + index],
                device_id=peer(0, 0),
                device_id_type=MESH,
            )
            copy.wait_send()
            copy.wait_recv()

        @pl.when(jnp.logical_not(inside(0, dy)))
        def _():
            reflect_rows(cor_in.at[index], cor_in.at[index], dy < 0, FLIP_Y)

        @pl.when(jnp.logical_not(inside(dx, 0)))
        def _():
            block = cor_in[index]
            turned = block
            for j in range(max(DEPTHS)):
                if dx < 0:
                    moved = pltpu.roll(block, LANES - 1 - 2 * j, 1)
                    turned = jnp.where(lane == LANES - 1 - j, moved, turned)
                else:
                    moved = pltpu.roll(block, 2 * j + 1, 1)
                    turned = jnp.where(lane == j, moved, turned)
            cor_in[index] = turned * flip_signs((PACK, LANES), FLIP_X)

    gap = jnp.zeros((half - PACK, LANES), jnp.float32)
    for b in range(side // LANES):
        cs = slice(b * LANES, (b + 1) * LANES)
        rs = slice(SUB + b * LANES, SUB + (b + 1) * LANES)
        halo = jnp.concatenate([col_in[1, :, cs], gap, col_in[0, :, cs], gap], 0).T
        for field, seam in enumerate(SEAMS):
            moved = pltpu.roll(halo, (LANES + quart - seam) % LANES, 1)
            ext[field, rs, seam_zone] = jnp.where(
                (lane_b >= quart) & (lane_b < LANES - quart), moved, ext[field, rs, seam_zone]
            )
    for i in range(2):
        first, last = row_in[i, :, 0:LANES], row_in[i, :, width - LANES : width]
        west, east = cor_in[2 * i], cor_in[2 * i + 1]
        cor_in[2 * i] = jnp.where(
            lane < half,
            pltpu.roll(jnp.where(lane < half, east, last), quart, 1),
            pltpu.roll(jnp.where(lane < half, first, west), LANES - quart, 1),
        )
    for field, (seam, depth) in enumerate(zip(SEAMS, DEPTHS)):
        north, south = slice(seam - depth, seam), slice(seam, seam + depth)
        top, end = slice(SUB - depth, SUB), slice(SUB + side, SUB + side + depth)
        ext[field, top, main_zone] = row_in[0, north, :]
        ext[field, end, main_zone] = row_in[1, south, :]
        ext[field, top, seam_zone] = cor_in[0, north, :]
        ext[field, end, seam_zone] = cor_in[2, south, :]

    for depth, stage in enumerate((stage_one, stage_two, stage_three, stage_four)):
        low = 1 if stage is stage_four else 0
        for k in range(depth + 1 - low):
            stage((k + low) * SUB, SUB, main_zone)
            stage((chunks - 1 - k - low) * SUB, SUB, main_zone)
    tall = chunks // 2
    run(
        (
            (6, stage_four, 0, tall),
            (4, stage_three, 0, tall),
            (2, stage_two, 0, tall),
            (0, stage_one, 0, tall),
        ),
        2 * SUB,
        seam_zone,
    )
    reach = max(DEPTHS)
    for b in range(side // LANES):
        rs = slice(b * LANES, (b + 1) * LANES)
        found = grad[SUB + b * LANES : SUB + (b + 1) * LANES, seam_zone]
        grad_out[rs, 0:LANES] = jnp.where(
            lane_b < reach, pltpu.roll(found, quart, 1), grad_out[rs, 0:LANES]
        )
        grad_out[rs, width - LANES : width] = jnp.where(
            lane_b >= LANES - reach,
            pltpu.roll(found, LANES - quart, 1),
            grad_out[rs, width - LANES : width],
        )


def on_device(n_gx, n_gy, water_state, ground, log_rough, moment, second, wet_tiles, cotangent):
    side, width = ground.shape
    ring = width + LANES
    rows = side + 2 * SUB
    tall = rows + 2 * SUB
    f32 = jnp.float32
    in_hbm = pl.BlockSpec(memory_space=pltpu.HBM)
    gradient = pl.pallas_call(
        functools.partial(kernel, n_gx, n_gy),
        out_shape=pltpu.VMEM((side, width), f32),
        in_specs=[in_hbm] * 5,
        out_specs=pl.BlockSpec(memory_space=pltpu.VMEM),
        scratch_shapes=[
            pltpu.SMEM(wet_tiles.shape, jnp.int32),
            pltpu.VMEM((8, rows, ring), f32),
            pltpu.VMEM((side, width), f32),
            pltpu.VMEM((PACK, side), f32),
            pltpu.VMEM((PACK, width), f32),
            pltpu.VMEM((PACK, LANES), f32),
            pltpu.VMEM((2, PACK, side), f32),
            pltpu.VMEM((2, PACK, width), f32),
            pltpu.VMEM((4, PACK, LANES), f32),
            pltpu.VMEM((2, rows, ring), f32),
            pltpu.VMEM((2, 3, rows, ring), f32),
            pltpu.VMEM((2, 4, tall, ring), f32),
            pltpu.VMEM((2, 3, tall, ring), f32),
            pltpu.VMEM((3, rows, ring), f32),
            pltpu.VMEM((rows, ring), f32),
            pltpu.VMEM((2, rows, ring), f32),
            pltpu.VMEM((3, tall, ring), f32),
            pltpu.VMEM((rows, ring), f32),
            pltpu.SemaphoreType.DMA((5,)),
            pltpu.SemaphoreType.DMA((8,)),
            pltpu.SemaphoreType.DMA((8,)),
        ],
        compiler_params=pltpu.CompilerParams(
            collective_id=0, has_side_effects=True, vmem_limit_bytes=LIMIT * 1024 * 1024
        ),
        name="flood_gradient",
    )(water_state, ground, log_rough, wet_tiles, cotangent)
    new_moment = BETA_ONE * moment + (1.0 - BETA_ONE) * gradient
    new_second = BETA_TWO * second + (1.0 - BETA_TWO) * gradient * gradient
    direction = jnp.arctan2(
        new_moment / (1.0 - BETA_ONE**UPDATES), jnp.sqrt(new_second / (1.0 - BETA_TWO**UPDATES))
    )
    new_rough = log_rough - LEARN_RATE * ATAN_SCALE * direction
    return (new_rough, new_moment, new_second)


def solution(mesh):
    field, plane = P(None, "gy", "gx"), P("gy", "gx")
    return jax.shard_map(
        functools.partial(on_device, mesh.shape["gx"], mesh.shape["gy"]),
        mesh=mesh,
        in_specs=(field, plane, plane, plane, plane, plane, field),
        out_specs=(plane, plane, plane),
        check_vma=False,
    )
```

```python
import functools

import jax
import jax.numpy as jnp
from jax import lax
from jax.experimental import pallas as pl
from jax.experimental.pallas import tpu as pltpu
from jax.sharding import PartitionSpec as P

UPDATES = 20
GRAVITY = 9.81
HALF_STEP = 0.05
GRAVITY_DT = 9.81
SPEED_EPS = 0.0001
BETA_ONE = 0.9
BETA_TWO = 0.999
LEARN_RATE = 0.05
ATAN_SCALE = 1.27

MESH = pl.DeviceIdType.MESH
DEPTHS = (3, 3, 3, 3, 2, 1, 1, 1)
SEAMS = (3, 9, 15, 21, 26, 29, 31, 33)
PACK = 40
LIMIT = 62
FLIP_X = (1, 6)
FLIP_Y = (2, 7)
LANES = 128
SUB = 8
CORNERS = ((-1, -1), (1, -1), (-1, 1), (1, 1))


def flip_signs(shape, flipped):
    rows = lax.broadcasted_iota(jnp.int32, shape, 0)
    mask = jnp.zeros(shape, jnp.bool_)
    for field in flipped:
        seam, depth = SEAMS[field], DEPTHS[field]
        mask = mask | ((rows >= seam - depth) & (rows < seam + depth))
    return jnp.where(mask, -1.0, 1.0)


def reflect_rows(src, dst, low, flipped):
    for field, (seam, depth) in enumerate(zip(SEAMS, DEPTHS)):
        sign = -1.0 if field in flipped else 1.0
        for j in range(depth):
            a, b = (seam - 1 - j, seam + j) if low else (seam + j, seam - 1 - j)
            dst[a : a + 1, :] = sign * src[b : b + 1, :]


def inverse(x):
    guess = pl.reciprocal(x, approx=True)
    return guess * (2.0 - x * guess)


def flux_parts(depth, east, south):
    inv = inverse(depth)
    u, v = east * inv, south * inv
    press = (0.5 * GRAVITY) * depth * depth
    qh, qe, qs = 0.25 * depth, 0.25 * east, 0.25 * south
    a0 = HALF_STEP * east
    a1 = HALF_STEP * (east * u + press)
    a2 = HALF_STEP * (east * v)
    b0 = HALF_STEP * south
    b2 = HALF_STEP * (south * v + press)
    return u, v, (qh, qe, qs), (a0, a1, a2), (b0, a2, b2)


def kernel(
    n_gx,
    n_gy,
    water,
    ground,
    rough,
    wet_tiles,
    cot,
    grad_out,
    wet,
    ext,
    rough_v,
    colpk,
    rowpk,
    corpk,
    col_in,
    row_in,
    cor_in,
    slopes,
    mix,
    rise,
    fall,
    state,
    damp,
    vel,
    lam,
    grad,
    load_sem,
    send_sem,
    recv_sem,
):
    side = rough.shape[0]
    width = rough.shape[1]
    tile_rows, tile_cols = wet.shape
    tile_h, tile_w = side // tile_rows, width // tile_cols
    ring = width + LANES
    chunks = side // SUB + 2
    gx = lax.axis_index("gx")
    gy = lax.axis_index("gy")

    def inside(dx, dy):
        checks = []
        if dx < 0:
            checks.append(gx > 0)
        if dx > 0:
            checks.append(gx < n_gx - 1)
        if dy < 0:
            checks.append(gy > 0)
        if dy > 0:
            checks.append(gy < n_gy - 1)
        return functools.reduce(jnp.logical_and, checks)

    def peer(dx, dy):
        return {"gx": gx + dx, "gy": gy + dy}

    loads = [
        pltpu.make_async_copy(water, ext.at[0:3, SUB : SUB + side, 0:width], load_sem.at[0]),
        pltpu.make_async_copy(rough, rough_v, load_sem.at[1]),
        pltpu.make_async_copy(ground, ext.at[3, SUB : SUB + side, 0:width], load_sem.at[2]),
        pltpu.make_async_copy(cot, ext.at[5:8, SUB : SUB + side, 0:width], load_sem.at[3]),
        pltpu.make_async_copy(wet_tiles, wet, load_sem.at[4]),
    ]
    for load in loads:
        load.start()

    barrier = pltpu.get_barrier_semaphore()
    around = [(dx, dy) for dx in (-1, 0, 1) for dy in (-1, 0, 1) if (dx, dy) != (0, 0)]
    count = jnp.int32(0)
    for dx, dy in around:
        ok = inside(dx, dy)

        @pl.when(ok)
        def _():
            pl.semaphore_signal(barrier, inc=1, device_id=peer(dx, dy), device_id_type=MESH)

        count = count + ok.astype(jnp.int32)

    for load in loads:
        load.wait()
    for i in range(tile_rows):
        for j in range(tile_cols):
            rs, cs = slice(i * tile_h, (i + 1) * tile_h), slice(j * tile_w, (j + 1) * tile_w)
            coef = GRAVITY_DT * jnp.exp(2.0 * rough_v[rs, cs])
            ext[4, SUB + i * tile_h : SUB + (i + 1) * tile_h, cs] = jnp.where(
                wet[i, j] > 0, coef, -1.0
            )

    lane_b = lax.broadcasted_iota(jnp.int32, (LANES, LANES), 1)
    for b in range(side // LANES):
        packed = jnp.zeros((LANES, LANES), jnp.float32)
        rs = slice(SUB + b * LANES, SUB + (b + 1) * LANES)
        for field, (seam, depth) in enumerate(zip(SEAMS, DEPTHS)):
            both = jnp.where(
                lane_b < LANES // 2, ext[field, rs, 0:LANES], ext[field, rs, width - LANES : width]
            )
            both = pltpu.roll(both, seam, 1)
            packed = jnp.where((lane_b >= seam - depth) & (lane_b < seam + depth), both, packed)
        colpk[:, b * LANES : (b + 1) * LANES] = packed.T[0:PACK]

    pl.semaphore_wait(barrier, count)

    def straight(dx, dy, out_slot, in_slot):
        src, dst = (colpk, col_in) if dx else (rowpk, row_in)
        return pltpu.make_async_remote_copy(
            src_ref=src,
            dst_ref=dst.at[in_slot % 2],
            send_sem=send_sem.at[out_slot],
            recv_sem=recv_sem.at[in_slot],
            device_id=peer(dx, dy),
            device_id_type=MESH,
        )

    straights = [(-1, 0, 0, 1), (1, 0, 1, 0), (0, -1, 2, 3), (0, 1, 3, 2)]

    def corner(dx, dy, in_x, in_y, index):
        slot = CORNERS.index((-dx if in_x else dx, -dy if in_y else dy))
        return pltpu.make_async_remote_copy(
            src_ref=corpk,
            dst_ref=cor_in.at[slot],
            send_sem=send_sem.at[4 + index],
            recv_sem=recv_sem.at[4 + slot],
            device_id=peer(dx if in_x else 0, dy if in_y else 0),
            device_id_type=MESH,
        )

    def corner_cases(index):
        dx, dy = CORNERS[index]
        ok_x, ok_y = inside(dx, 0), inside(0, dy)
        no_x, no_y = jnp.logical_not(ok_x), jnp.logical_not(ok_y)
        return [
            (ok_x & ok_y, corner(dx, dy, True, True, index)),
            (ok_x & no_y, corner(dx, dy, True, False, index)),
            (no_x & ok_y, corner(dx, dy, False, True, index)),
        ]

    for args in straights[:2]:

        @pl.when(inside(args[0], args[1]))
        def _():
            straight(*args).start()

    for field, (seam, depth) in enumerate(zip(SEAMS, DEPTHS)):
        rowpk[seam - depth : seam, :] = ext[field, SUB + side - depth : SUB + side, 0:width]
        rowpk[seam : seam + depth, :] = ext[field, SUB : SUB + depth, 0:width]
    lane = lax.broadcasted_iota(jnp.int32, (PACK, LANES), 1)
    corpk[...] = jnp.where(lane < LANES // 2, rowpk[:, 0:LANES], rowpk[:, width - LANES : width])
    for args in straights[2:]:

        @pl.when(inside(args[0], args[1]))
        def _():
            straight(*args).start()

    for index in range(4):
        for ok, copy in corner_cases(index):

            @pl.when(ok)
            def _():
                copy.start()

        dx, dy = CORNERS[index]

        @pl.when(jnp.logical_not(inside(dx, 0) | inside(0, dy)))
        def _():
            cor_in[index] = corpk[...]

    for slot, (dx, dy) in enumerate(((-1, 0), (1, 0), (0, -1), (0, 1))):

        @pl.when(jnp.logical_not(inside(dx, dy)))
        def _():
            if dx:
                reflect_rows(colpk, col_in.at[slot % 2], dx < 0, FLIP_X)
            else:
                reflect_rows(rowpk, row_in.at[slot % 2], dy < 0, FLIP_Y)

    def beside(ref, lead, at, rows, zone, shift):
        view = ref.at[lead + (pl.ds(at, rows + 2 * SUB),)]
        return view[SUB + shift : SUB + rows + shift, zone]

    def east_of(array):
        return pltpu.roll(array, array.shape[1] - 1, 1)

    def west_of(array):
        return pltpu.roll(array, 1, 1)

    def spread(step, at, rows, zone, values):
        here, inner = pl.ds(at, rows), pl.ds(at + SUB, rows)
        u, v, quarter, a, b = flux_parts(*values)
        for f in range(3):
            mix[step, f, here, zone] = east_of(quarter[f] - a[f]) + west_of(quarter[f] + a[f])
            rise[step, f, inner, zone] = quarter[f] - b[f]
            fall[step, f, inner, zone] = quarter[f] + b[f]
        return u, v

    def gather(step, at, rows, zone, depth, slope_x, slope_y):
        pre = [
            mix[step, f, pl.ds(at, rows), zone]
            + beside(rise, (step, f), at, rows, zone, 1)
            + beside(fall, (step, f), at, rows, zone, -1)
            for f in range(3)
        ]
        return pre[0], pre[1] - depth * slope_x, pre[2] - depth * slope_y

    def drag_of(coef, pre):
        depth, east, south = pre
        square = east * east + south * south + SPEED_EPS
        inv_speed = lax.rsqrt(square)
        power = jnp.exp((-7.0 / 3.0) * jnp.log(depth))
        extra = coef * (square * inv_speed) * power
        return extra, inverse(1.0 + extra), inv_speed * inv_speed

    def stage_one(at, rows, zone):
        here = pl.ds(at, rows)
        z = (HALF_STEP * GRAVITY) * ext[3, here, zone]
        slopes[0, here, zone] = east_of(z) - west_of(z)
        rise[0, 3, pl.ds(at + SUB, rows), zone] = z
        spread(0, at, rows, zone, [ext[f, here, zone] for f in range(3)])

    def stage_two(at, rows, zone):
        here = pl.ds(at, rows)
        depth, east, south = [ext[f, here, zone] for f in range(3)]
        slope_y = beside(rise, (0, 3), at, rows, zone, 1) - beside(rise, (0, 3), at, rows, zone, -1)
        slopes[1, here, zone] = slope_y
        pre = gather(0, at, rows, zone, depth, slopes[0, here, zone], slope_y)
        coef = ext[4, here, zone]
        is_wet = coef > 0
        extra, inv, _ = drag_of(coef, pre)
        now = [
            jnp.where(is_wet, pre[0], depth),
            jnp.where(is_wet, pre[1] * inv, east),
            jnp.where(is_wet, pre[2] * inv, south),
        ]
        damp[here, zone] = extra * inv
        for f in range(3):
            state[f, here, zone] = now[f]
        u, v = spread(1, at, rows, zone, now)
        vel[0, here, zone] = u
        vel[1, here, zone] = v

    def stage_three(at, rows, zone):
        here = pl.ds(at, rows)
        pre = gather(1, at, rows, zone, state[0, here, zone], slopes[0, here, zone], slopes[1, here, zone])
        coef = ext[4, here, zone]
        is_wet = coef > 0
        extra, inv, inv_square = drag_of(coef, pre)
        c_depth, c_east, c_south = [ext[5 + f, here, zone] for f in range(3)]
        t = -(c_east * pre[1] + c_south * pre[2]) * (inv * inv * extra)
        inner = pl.ds(at + SUB, rows)
        tq = t * inv_square
        lam[0, inner, zone] = jnp.where(is_wet, c_depth - (7.0 / 3.0) * t * inverse(pre[0]), 0.0)
        lam[1, inner, zone] = jnp.where(is_wet, c_east * inv + tq * pre[1], 0.0)
        lam[2, inner, zone] = jnp.where(is_wet, c_south * inv + tq * pre[2], 0.0)
        grad[here, zone] = t

    def stage_four(at, rows, zone):
        here = pl.ds(at, rows)
        mean, dx, dy = [], [], []
        for f in range(3):
            mid = lam[f, pl.ds(at + SUB, rows), zone]
            east, west = east_of(mid), west_of(mid)
            south = beside(lam, (f,), at, rows, zone, 1)
            north = beside(lam, (f,), at, rows, zone, -1)
            if f:
                mean.append(0.25 * ((east + west) + (south + north)))
            dx.append(HALF_STEP * (east - west))
            dy.append(HALF_STEP * (south - north))
        u, v = vel[0, here, zone], vel[1, here, zone]
        cross = dx[2] + dy[1]
        a_east = mean[0] + dx[0] + 2.0 * u * dx[1] + v * cross
        a_south = mean[1] + dy[0] + 2.0 * v * dy[2] + u * cross
        total = grad[here, zone] - (
            a_east * state[1, here, zone] + a_south * state[2, here, zone]
        ) * damp[here, zone]
        result = jnp.where(ext[4, here, zone] > 0, 2.0 * total, 0.0)
        if zone is seam_zone:
            grad[here, zone] = result
        else:
            out = at - SUB
            out = out if isinstance(out, int) else pl.multiple_of(out, SUB)
            grad_out[pl.ds(out, rows), :] = result

    def run(stages, rows, zone):
        def turn(i):
            for lag, stage, low, high in stages:
                if not isinstance(i, int):
                    stage(pl.multiple_of((i - lag) * rows, SUB), rows, zone)
                elif low <= i - lag < high:
                    stage((i - lag) * rows, rows, zone)

        def body(j, carry):
            turn(full + 2 * j)
            turn(full + 2 * j + 1)
            return carry

        begin = min(lag + low for lag, _, low, _ in stages)
        full = max(lag + low for lag, _, low, _ in stages)
        drain = min(lag + high for lag, _, _, high in stages)
        end = max(lag + high for lag, _, _, high in stages)
        for i in range(begin, full):
            turn(i)
        pairs = (drain - full) // 2
        lax.fori_loop(0, pairs, body, 0)
        for i in range(full + 2 * pairs, end):
            turn(i)

    main_zone, seam_zone = slice(0, width), slice(width, ring)
    half, quart = LANES // 2, LANES // 4
    for b in range(side // LANES):
        rs = slice(SUB + b * LANES, SUB + (b + 1) * LANES)
        for field in range(8):
            ext[field, rs, seam_zone] = jnp.where(
                lane_b < half,
                pltpu.roll(ext[field, rs, width - LANES : width], quart, 1),
                pltpu.roll(ext[field, rs, 0:LANES], LANES - quart, 1),
            )
    run(
        (
            (6, stage_four, 4, chunks - 4),
            (4, stage_three, 3, chunks - 3),
            (2, stage_two, 2, chunks - 2),
            (0, stage_one, 1, chunks - 1),
        ),
        SUB,
        main_zone,
    )

    for args in straights:

        @pl.when(inside(args[0], args[1]))
        def _():
            dx, dy, out_slot, _ = args
            back = straight(dx, dy, out_slot, out_slot)
            back.wait_send()
            back.wait_recv()

    for index in range(4):
        dx, dy = CORNERS[index]

        @pl.when(inside(dx, 0) | inside(0, dy))
        def _():
            copy = pltpu.make_async_remote_copy(
                src_ref=corpk,
                dst_ref=cor_in.at[index],
                send_sem=send_sem.at[4 + index],
                recv_sem=recv_sem.at[4 + index],
                device_id=peer(0, 0),
                device_id_type=MESH,
            )
            copy.wait_send()
            copy.wait_recv()

        @pl.when(jnp.logical_not(inside(0, dy)))
        def _():
            reflect_rows(cor_in.at[index], cor_in.at[index], dy < 0, FLIP_Y)

        @pl.when(jnp.logical_not(inside(dx, 0)))
        def _():
            block = cor_in[index]
            turned = block
            for j in range(max(DEPTHS)):
                if dx < 0:
                    moved = pltpu.roll(block, LANES - 1 - 2 * j, 1)
                    turned = jnp.where(lane == LANES - 1 - j, moved, turned)
                else:
                    moved = pltpu.roll(block, 2 * j + 1, 1)
                    turned = jnp.where(lane == j, moved, turned)
            cor_in[index] = turned * flip_signs((PACK, LANES), FLIP_X)

    gap = jnp.zeros((half - PACK, LANES), jnp.float32)
    for b in range(side // LANES):
        cs = slice(b * LANES, (b + 1) * LANES)
        rs = slice(SUB + b * LANES, SUB + (b + 1) * LANES)
        halo = jnp.concatenate([col_in[1, :, cs], gap, col_in[0, :, cs], gap], 0).T
        for field, seam in enumerate(SEAMS):
            moved = pltpu.roll(halo, (LANES + quart - seam) % LANES, 1)
            ext[field, rs, seam_zone] = jnp.where(
                (lane_b >= quart) & (lane_b < LANES - quart), moved, ext[field, rs, seam_zone]
            )
    for i in range(2):
        first, last = row_in[i, :, 0:LANES], row_in[i, :, width - LANES : width]
        west, east = cor_in[2 * i], cor_in[2 * i + 1]
        cor_in[2 * i] = jnp.where(
            lane < half,
            pltpu.roll(jnp.where(lane < half, east, last), quart, 1),
            pltpu.roll(jnp.where(lane < half, first, west), LANES - quart, 1),
        )
    for field, (seam, depth) in enumerate(zip(SEAMS, DEPTHS)):
        north, south = slice(seam - depth, seam), slice(seam, seam + depth)
        top, end = slice(SUB - depth, SUB), slice(SUB + side, SUB + side + depth)
        ext[field, top, main_zone] = row_in[0, north, :]
        ext[field, end, main_zone] = row_in[1, south, :]
        ext[field, top, seam_zone] = cor_in[0, north, :]
        ext[field, end, seam_zone] = cor_in[2, south, :]

    for depth, stage in enumerate((stage_one, stage_two, stage_three, stage_four)):
        low = 1 if stage is stage_four else 0
        for k in range(depth + 1 - low):
            stage((k + low) * SUB, SUB, main_zone)
            stage((chunks - 1 - k - low) * SUB, SUB, main_zone)
    tall = chunks // 2
    run(
        (
            (6, stage_four, 0, tall),
            (4, stage_three, 0, tall),
            (2, stage_two, 0, tall),
            (0, stage_one, 0, tall),
        ),
        2 * SUB,
        seam_zone,
    )
    reach = max(DEPTHS)
    for b in range(side // LANES):
        rs = slice(b * LANES, (b + 1) * LANES)
        found = grad[SUB + b * LANES : SUB + (b + 1) * LANES, seam_zone]
        grad_out[rs, 0:LANES] = jnp.where(
            lane_b < reach, pltpu.roll(found, quart, 1), grad_out[rs, 0:LANES]
        )
        grad_out[rs, width - LANES : width] = jnp.where(
            lane_b >= LANES - reach,
            pltpu.roll(found, LANES - quart, 1),
            grad_out[rs, width - LANES : width],
        )


def on_device(n_gx, n_gy, water_state, ground, log_rough, moment, second, wet_tiles, cotangent):
    side, width = ground.shape
    ring = width + LANES
    rows = side + 2 * SUB
    tall = rows + 2 * SUB
    f32 = jnp.float32
    in_hbm = pl.BlockSpec(memory_space=pltpu.HBM)
    gradient = pl.pallas_call(
        functools.partial(kernel, n_gx, n_gy),
        out_shape=pltpu.VMEM((side, width), f32),
        in_specs=[in_hbm] * 5,
        out_specs=pl.BlockSpec(memory_space=pltpu.VMEM),
        scratch_shapes=[
            pltpu.SMEM(wet_tiles.shape, jnp.int32),
            pltpu.VMEM((8, rows, ring), f32),
            pltpu.VMEM((side, width), f32),
            pltpu.VMEM((PACK, side), f32),
            pltpu.VMEM((PACK, width), f32),
            pltpu.VMEM((PACK, LANES), f32),
            pltpu.VMEM((2, PACK, side), f32),
            pltpu.VMEM((2, PACK, width), f32),
            pltpu.VMEM((4, PACK, LANES), f32),
            pltpu.VMEM((2, rows, ring), f32),
            pltpu.VMEM((2, 3, rows, ring), f32),
            pltpu.VMEM((2, 4, tall, ring), f32),
            pltpu.VMEM((2, 3, tall, ring), f32),
            pltpu.VMEM((3, rows, ring), f32),
            pltpu.VMEM((rows, ring), f32),
            pltpu.VMEM((2, rows, ring), f32),
            pltpu.VMEM((3, tall, ring), f32),
            pltpu.VMEM((rows, ring), f32),
            pltpu.SemaphoreType.DMA((5,)),
            pltpu.SemaphoreType.DMA((8,)),
            pltpu.SemaphoreType.DMA((8,)),
        ],
        compiler_params=pltpu.CompilerParams(
            collective_id=0, has_side_effects=True, vmem_limit_bytes=LIMIT * 1024 * 1024
        ),
        name="flood_gradient",
    )(water_state, ground, log_rough, wet_tiles, cotangent)
    new_moment = BETA_ONE * moment + (1.0 - BETA_ONE) * gradient
    new_second = BETA_TWO * second + (1.0 - BETA_TWO) * gradient * gradient
    direction = jnp.arctan2(
        new_moment / (1.0 - BETA_ONE**UPDATES), jnp.sqrt(new_second / (1.0 - BETA_TWO**UPDATES))
    )
    new_rough = log_rough - LEARN_RATE * ATAN_SCALE * direction
    return (new_rough, new_moment, new_second)


def solution(mesh):
    field, plane = P(None, "gy", "gx"), P("gy", "gx")
    return jax.shard_map(
        functools.partial(on_device, mesh.shape["gx"], mesh.shape["gy"]),
        mesh=mesh,
        in_specs=(field, plane, plane, plane, plane, plane, field),
        out_specs=(plane, plane, plane),
        check_vma=False,
    )
```
